32 devices in a mesh: dp: 8 (over z, x), slab: 4 (over y, core).
Axes of the slice: x: 2, y: 2, z: 4, core: 2. Of those that a mesh axis runs over, the one named last changes fastest.
Arguments:
- inputs: bfloat16 [8, 24, 34944], P('dp', 'slab'), may hold values from -40 to 40
- upstream: bfloat16 [8, 24, 34944], P('dp', 'slab'), may hold values from -96 to 96
- labels: int32 [8, 24, 48], P('dp', 'slab'), may hold values from 0 to 2
- class_weights: float32 [3], replicated, may hold values from 0.25 to 4
- depth_kernel: bfloat16 [9, 728], replicated, may hold values from -2 to 2
- point_weight: bfloat16 [728, 728], replicated, may hold values from -0.21875 to 0.21875
- gain: float32 [728], replicated, may hold values from 0.5 to 1.5
- shift: float32 [728], replicated, may hold values from -3 to 3
Outputs:
- block_out: bfloat16 [8, 24, 34944], P('dp', 'slab')
- grad_input: bfloat16 [8, 24, 34944], P('dp', 'slab')
- grad_pointwise: float32 [728, 728], P(None, 'slab')
- grad_depthwise: float32 [9, 728], P(None, 'slab')
- grad_gain: float32 [728], P('slab')
- grad_shift: float32 [728], P('slab')
The draws below stay inside these ranges and needn't reach their ends.
All inputs are finite; a program needn't handle non-finite values.
Results may differ from the reference program's by a relative error of at most 0.0052.
The reference program's roundings to bfloat16 on the way (of `active`, `depth`, `grad_proj` and `grad_depth`) count: a program that leaves them out, or rounds other values in their place, can miss the bound.
Values may be sent and summed in bfloat16 or wider, within the bound.
No kernel may reach another device: no remote copies, remote signals or barrier semaphores. Data moves between devices by JAX's collectives and lax.ppermute only.
A program may use at most 64 MiB of HBM per device.

```python
import math
import jax
import jax.numpy as jnp
from jax import lax

CH = 728
WIDTH = 48
SAMP_DEV = 1
BATCH = 8
HEIGHT = 24
N_DP = 8


def rise_profile():
    return 3.0 ** (jnp.arange(HEIGHT, dtype=jnp.float32) / max(HEIGHT - 1, 1))


def draw_inputs(key, part):
    first = jax.random.fold_in(jax.random.fold_in(key, 11), 0)
    third = jax.random.fold_in(jax.random.fold_in(key, 11), 2)
    base = jax.random.normal(first, (BATCH, HEIGHT, WIDTH, CH), jnp.float32)
    rough = jnp.exp(jax.random.uniform(third, (BATCH, HEIGHT, WIDTH, 1), jnp.float32, -0.5 * math.log(2.0), 0.5 * math.log(2.0)))
    values = jnp.clip(base * rough * rise_profile()[None, :, None, None], -40.0, 40.0)
    return values.reshape(BATCH, HEIGHT, WIDTH * CH).astype(jnp.bfloat16)


def draw_upstream(key, part):
    first = jax.random.fold_in(jax.random.fold_in(key, 23), 0)
    third = jax.random.fold_in(jax.random.fold_in(key, 23), 2)
    fourth = jax.random.fold_in(key, 37)
    base = jax.random.normal(first, (BATCH, HEIGHT, WIDTH, CH), jnp.float32)
    rough = jnp.exp(jax.random.uniform(third, (BATCH, HEIGHT, WIDTH, 1), jnp.float32, -0.5 * math.log(2.0), 0.5 * math.log(2.0)))
    partner = jax.random.permutation(fourth, BATCH)
    channel_slot = jnp.arange(CH, dtype=jnp.int32) % BATCH
    heavy = jnp.where(channel_slot[None, :] == partner[:, None], 8.0, 1.0).astype(jnp.float32)
    values = base * rough * rise_profile()[None, :, None, None] * heavy[:, None, None, :]
    values = jnp.clip(values, -96.0, 96.0)
    return values.reshape(BATCH, HEIGHT, WIDTH * CH).astype(jnp.bfloat16)


def plant(entries, rng, low, largest):
    longest = entries.shape.index(max(entries.shape))
    spots = []
    for shift in (0, 1):
        where = [jax.random.randint(jax.random.fold_in(rng, axis), (), 0, length) for axis, length in enumerate(entries.shape)]
        where[longest] = (where[longest] + shift) % entries.shape[longest]
        spots.append(tuple(where))
    return entries.at[spots[0]].set(low).at[spots[1]].set(largest)


def normal_values(key, extent, scale, most, kind=jnp.bfloat16):
    return jnp.clip(scale * jax.random.normal(key, extent, jnp.float32), -most, most).astype(kind)


def setup_inputs(seed: int = 0) -> dict:
    splits = jax.random.split(jax.random.key(seed), 9)
    inputs = draw_inputs(jax.random.fold_in(splits[8], 71), 0)
    upstream = draw_upstream(jax.random.fold_in(splits[8], 71), 0)
    labels = plant(jax.random.randint(splits[2], (BATCH, HEIGHT, WIDTH), 0, 3), jax.random.fold_in(splits[2], 1), 0, 2).astype(jnp.int32)
    class_weights = jnp.clip(jnp.exp(jax.random.uniform(splits[3], (3,), jnp.float32, math.log(0.25), math.log(4.0))), 0.25, 4.0)
    depth_kernel = normal_values(splits[4], (9, CH), 9 ** -0.5, 2.0)
    point_weight = normal_values(splits[5], (CH, CH), CH ** -0.5, 0.21875)
    gain = jnp.clip(1.0 + 0.1 * jax.random.normal(splits[6], (CH,), jnp.float32), 0.5, 1.5)
    shift = normal_values(splits[7], (CH,), 0.5, 3.0, jnp.float32)
    return dict(inputs=inputs, upstream=upstream, labels=labels, class_weights=class_weights, depth_kernel=depth_kernel, point_weight=point_weight, gain=gain, shift=shift)


def widen_columns(values):
    return jnp.pad(values, ((0, 0), (0, 0), (1, 1), (0, 0)))

def depthwise(padded, kernel):
    row_count = padded.shape[1] - 2
    col_count = padded.shape[2]
    widened = widen_columns(padded)
    summed = jnp.zeros((padded.shape[0], row_count, col_count, padded.shape[3]), jnp.float32)
    for row_tap in range(3):
        for col_tap in range(3):
            window = widened[:, row_tap:row_tap + row_count, col_tap:col_tap + col_count, :]
            summed = summed + window.astype(jnp.float32) * kernel[3 * row_tap + col_tap].astype(jnp.float32)
    return summed

def transposed(padded_grad, kernel):
    row_count = padded_grad.shape[1] - 2
    col_count = padded_grad.shape[2]
    widened = widen_columns(padded_grad)
    summed = jnp.zeros((padded_grad.shape[0], row_count, col_count, padded_grad.shape[3]), jnp.float32)
    for row_tap in range(3):
        for col_tap in range(3):
            window = widened[:, 2 - row_tap:2 - row_tap + row_count, 2 - col_tap:2 - col_tap + col_count, :]
            summed = summed + window.astype(jnp.float32) * kernel[3 * row_tap + col_tap].astype(jnp.float32)
    return summed

def taps(padded, grad_image):
    row_count = grad_image.shape[1]
    col_count = grad_image.shape[2]
    widened = widen_columns(padded)
    results = []
    for row_tap in range(3):
        for col_tap in range(3):
            window = widened[:, row_tap:row_tap + row_count, col_tap:col_tap + col_count, :]
            results.append(jnp.einsum('srwc,srwc->c', window.astype(jnp.float32), grad_image.astype(jnp.float32), precision=lax.Precision.HIGHEST))
    return jnp.stack(results)

def reference(inputs, upstream, labels, class_weights, depth_kernel, point_weight, gain, shift):
    image = inputs.reshape(N_DP, SAMP_DEV, HEIGHT, WIDTH, CH)
    cotangent = upstream.reshape(N_DP, SAMP_DEV, HEIGHT, WIDTH, CH)
    classes = labels.reshape(N_DP, SAMP_DEV * HEIGHT * WIDTH)

    def group_step(running, group_items):
        sample, incoming, label_group = group_items
        active = jnp.maximum(sample, 0)
        padded = jnp.pad(active, ((0, 0), (1, 1), (0, 0), (0, 0)))
        depth = depthwise(padded, depth_kernel).astype(jnp.bfloat16)
        flat_depth = depth.reshape(-1, CH)
        projected = jnp.dot(flat_depth, point_weight, preferred_element_type=jnp.float32)
        center = lax.optimization_barrier(jnp.mean(projected, axis=0))
        spread = lax.optimization_barrier(jnp.mean((projected - center) ** 2, axis=0))
        inverse = lax.rsqrt(spread + 1e-05)
        normed = (projected - center) * inverse
        result = sample.reshape(-1, CH).astype(jnp.float32) + gain * normed + shift
        match = label_group[:, None] == jnp.arange(3, dtype=jnp.int32)[None, :]
        weight = lax.optimization_barrier(jnp.sum(jnp.where(match, class_weights[None, :], 0.0), axis=1))
        grad_out = incoming.reshape(-1, CH).astype(jnp.float32) * weight[:, None]
        count = projected.shape[0]
        shift_part = lax.optimization_barrier(jnp.sum(grad_out, axis=0))
        gain_part = lax.optimization_barrier(jnp.sum(grad_out * normed, axis=0))
        grad_proj = (gain * inverse * (grad_out - shift_part / count - normed * gain_part / count)).astype(jnp.bfloat16)
        grad_depth = jnp.dot(grad_proj, point_weight.T, preferred_element_type=jnp.float32).astype(jnp.bfloat16)
        point_part = jnp.dot(flat_depth.T, grad_proj, preferred_element_type=jnp.float32)
        grad_image = grad_depth.reshape(depth.shape)
        padded_grad = jnp.pad(grad_image, ((0, 0), (1, 1), (0, 0), (0, 0)))
        grad_active = transposed(padded_grad, depth_kernel).reshape(-1, CH)
        grad_input = grad_out + jnp.where(sample.reshape(-1, CH) > 0, grad_active, 0.0)
        tap_part = taps(padded, grad_image)
        running = (running[0] + point_part, running[1] + tap_part, running[2] + gain_part, running[3] + shift_part)
        return (running, (result.astype(jnp.bfloat16), grad_input.astype(jnp.bfloat16)))
    start = (jnp.zeros((CH, CH), jnp.float32), jnp.zeros((9, CH), jnp.float32), jnp.zeros((CH,), jnp.float32), jnp.zeros((CH,), jnp.float32))
    totals, outputs = lax.scan(group_step, start, (image, cotangent, classes))
    block_out = outputs[0].reshape(BATCH, HEIGHT, WIDTH * CH)
    grad_input = outputs[1].reshape(BATCH, HEIGHT, WIDTH * CH)
    return (block_out, grad_input, totals[0] / BATCH, totals[1] / BATCH, totals[2] / BATCH, totals[3] / BATCH)
```

```python
import functools

import jax
import jax.numpy as jnp
from jax import lax
from jax.experimental import pallas as pl
from jax.experimental.pallas import tpu as pltpu
from jax.sharding import PartitionSpec as P

F32 = jnp.float32
BF16 = jnp.bfloat16
LANES = 128
SUB = 8
EPS = 1e-05


def round_up(value, unit):
    return -(-value // unit) * unit


def tiles(width):
    return [(start, min(LANES, width - start)) for start in range(0, width, LANES)]


def share_order(pieces):
    return [2 * j + parity for parity in range(2) for j in range(pieces // 2)]


def to_shares(values, pieces, padded):
    share = values.shape[1] // pieces
    gap = padded // pieces - share
    parts = []
    for owner in share_order(pieces):
        parts.append(values[:, owner * share : (owner + 1) * share])
        if gap:
            parts.append(jnp.zeros((values.shape[0], gap), values.dtype))
    return jnp.concatenate(parts, axis=1)


def from_shares(values, pieces, channels):
    share = channels // pieces
    slot = values.shape[1] // pieces
    order = share_order(pieces)
    parts = []
    for owner in range(pieces):
        start = order.index(owner) * slot
        parts.append(values[:, start : start + share])
    return jnp.concatenate(parts, axis=1)


def column(ref, col, channels):
    start = col * channels
    base = start // LANES * LANES
    off = start - base
    end = min(ref.shape[1], base + round_up(off + channels, LANES))
    return ref[:, base:end].astype(F32)[:, off : off + channels]


def prepare_kernel(pieces, weights, x_ref, u_ref, label_ref, kernel_ref, point_ref, image_ref, part_ref, grad_ref, group_ref, spread_ref):
    rows, cols = label_ref.shape
    channels = point_ref.shape[0]
    sub = image_ref.shape[1]
    padded = spread_ref.shape[1]
    share, slot = channels // pieces, padded // pieces
    out_col = lax.broadcasted_iota(jnp.int32, (channels, padded), 1)
    in_row = lax.broadcasted_iota(jnp.int32, (channels, padded), 0)
    place = out_col // slot
    inside = out_col - place * slot
    owner = jnp.where(place >= pieces // 2, 2 * place - pieces + 1, 2 * place)
    chosen = (in_row == owner * share + inside) & (inside < share)
    picks = jnp.where(chosen, 1.0, 0.0).astype(BF16)
    spread_ref[...] = jnp.dot(point_ref[...], picks, preferred_element_type=F32).astype(BF16)
    labels = label_ref[...]
    weight = jnp.where(labels == 0, weights[0], jnp.where(labels == 1, weights[1], jnp.where(labels == 2, weights[2], 0.0)))
    for col in range(cols):
        values = column(x_ref, col, channels)
        image_ref[col, :rows, :] = values
        image_ref[col, rows:, :] = jnp.zeros((sub - rows, channels), F32)
        grads = column(u_ref, col, channels) * weight[:, col : col + 1]
        grad_ref[col, :rows, :] = grads
        grad_ref[col, rows:, :] = jnp.zeros((sub - rows, channels), F32)
        group_ref[col * sub : col * sub + rows, :] = to_shares(grads, pieces, padded)
        group_ref[col * sub + rows : (col + 1) * sub, :] = jnp.zeros((sub - rows, padded), F32)
    for start, width in tiles(channels):
        at = pl.ds(start, width)
        taps = [kernel_ref[t : t + 1, at].astype(F32) for t in range(9)]
        before = jnp.zeros((sub, width), F32)
        pending = before
        for col in range(cols):
            mid = jnp.maximum(image_ref[col, :, at], 0.0)
            up = pltpu.roll(mid, 1, 0)
            down = pltpu.roll(mid, sub - 1, 0)
            sums = [taps[j] * up + taps[3 + j] * mid + taps[6 + j] * down for j in range(3)]
            if col:
                part_ref[col - 1, :, at] = pending + sums[2]
            pending = before + sums[1]
            before = sums[0]
        part_ref[cols - 1, :, at] = pending


def forward_kernel(pieces, where_ref, part_ref, image_ref, one_ref, two_ref, kernel_ref, spread_ref, group_ref, depth_ref, proj_ref, active_ref, stats_ref, sums_ref, rows):
    cols, sub, channels = part_ref.shape
    padded = spread_ref.shape[1]
    even = where_ref[0] % 2 == 0
    has_top = jnp.where(where_ref[0] > 0, 1.0, 0.0)
    has_bottom = jnp.where(where_ref[0] < pieces - 1, 1.0, 0.0)
    line = lax.broadcasted_iota(jnp.int32, (sub, channels), 0)
    wide = [
        jnp.where(line == 0, kernel_ref[j : j + 1, :].astype(F32), kernel_ref[6 + j : 7 + j, :].astype(F32))
        for j in range(3)
    ]
    for col in range(cols):
        one = jnp.maximum(column(one_ref, col, channels), 0.0)
        two = jnp.maximum(column(two_ref, col, channels), 0.0)
        top = jnp.where(even, two, one) * has_top
        bottom = jnp.where(even, one, two) * has_bottom
        own = jnp.maximum(image_ref[col], 0.0)
        active_ref[col] = jnp.where(line == rows, bottom, jnp.where(line == sub - 1, top, own))
        sums_ref[col] = jnp.where(line == 0, top, jnp.where(line == rows - 1, bottom, 0.0))
    for start, width in tiles(channels):
        at = pl.ds(start, width)
        inside = lax.broadcasted_iota(jnp.int32, (sub, width), 0) < rows
        taps = [w[:, start : start + width] for w in wide]
        before = jnp.zeros((sub, width), F32)
        pending = before
        for col in range(cols):
            halo = sums_ref[col, :, at]
            if col:
                sums_ref[col - 1, :, at] = jnp.where(inside, part_ref[col - 1, :, at] + pending + taps[2] * halo, 0.0)
            pending = before + taps[1] * halo
            before = taps[0] * halo
        sums_ref[cols - 1, :, at] = jnp.where(inside, part_ref[cols - 1, :, at] + pending, 0.0)
    depth = sums_ref[...].reshape(cols * sub, channels).astype(BF16)
    depth_ref[...] = depth
    proj_ref[...] = jnp.dot(depth, spread_ref[...], preferred_element_type=F32)
    count = rows * cols
    for start, width in tiles(padded):
        at = pl.ds(start, width)
        proj = proj_ref[:, at]
        grads = group_ref[:, at]
        mine = lax.broadcasted_iota(jnp.int32, (cols * sub, width), 0) % sub < rows
        center = jnp.sum(proj, axis=0, keepdims=True) / count
        deviation = jnp.where(mine, proj - center, 0.0)
        stats_ref[0:1, at] = center
        stats_ref[1:2, at] = jnp.sum(deviation * deviation, axis=0, keepdims=True)
        stats_ref[2:3, at] = jnp.sum(grads, axis=0, keepdims=True)
        stats_ref[3:4, at] = jnp.sum(grads * deviation, axis=0, keepdims=True)
        stats_ref[4:SUB, at] = jnp.zeros((SUB - 4, width), F32)


def cotangent_kernel(pieces, rows, cols, where_ref, stats_ref, proj_ref, group_ref, gain_ref, shift_ref, full_ref, keep_ref, send_ref, norm_ref):
    padded = proj_ref.shape[1]
    sub = proj_ref.shape[0] // cols
    local = rows * cols
    count = local * pieces
    stats = [stats_ref[p * SUB : p * SUB + 4, :] for p in range(pieces)]
    center = sum(s[0:1] for s in stats) / pieces
    square = sum(s[1:2] + local * (s[0:1] - center) ** 2 for s in stats)
    shift_part = sum(s[2:3] for s in stats)
    cross = sum(s[3:4] + (s[0:1] - center) * s[2:3] for s in stats)
    inverse = lax.rsqrt(square / count + EPS)
    gain_part = cross * inverse
    gain = to_shares(gain_ref[...], pieces, padded)
    norm_ref[0:1, :] = center
    norm_ref[1:2, :] = inverse
    norm_ref[2:3, :] = gain
    norm_ref[3:4, :] = to_shares(shift_ref[...], pieces, padded)
    norm_ref[4:5, :] = gain_part
    norm_ref[5:6, :] = shift_part
    norm_ref[6:8, :] = jnp.zeros((2, padded), F32)
    for start, width in tiles(padded):
        at = slice(start, start + width)
        mine = lax.broadcasted_iota(jnp.int32, (cols * sub, width), 0) % sub < rows
        normed = (proj_ref[:, start : start + width] - center[:, at]) * inverse[:, at]
        value = (gain * inverse)[:, at] * (
            group_ref[:, start : start + width] - (shift_part / count)[:, at] - normed * (gain_part / count)[:, at]
        )
        full_ref[:, start : start + width] = jnp.where(mine, value, 0.0).astype(BF16)
    even = where_ref[0] % 2 == 0
    half = padded // 2
    first, second = full_ref[:, :half], full_ref[:, half:]
    keep_ref[...] = jnp.where(even, first, second)
    send_ref[...] = jnp.where(even, second, first)


def backward_kernel(rows, full_ref, spread_ref, active_ref, where_ref, depth_grad_ref, tap_ref, one_ref, two_ref):
    cols, sub, channels = active_ref.shape
    grad = lax.dot_general(full_ref[...], spread_ref[...], (((1,), (1,)), ((), ())), preferred_element_type=F32)
    depth_grad_ref[...] = grad.astype(BF16).astype(F32).reshape(cols, sub, channels)
    even = where_ref[0] % 2 == 0
    first = depth_grad_ref[:, 0, :].astype(BF16)
    last = depth_grad_ref[:, rows - 1, :].astype(BF16)
    one_ref[...] = jnp.where(even, last, first)
    two_ref[...] = jnp.where(even, first, last)
    for start, width in tiles(channels):
        at = pl.ds(start, width)
        totals = [jnp.zeros((sub, width), F32) for _ in range(9)]
        zero = jnp.zeros((sub, width), F32)
        ahead = depth_grad_ref[0, :, at]
        here = zero
        for col in range(cols):
            behind, here = here, ahead
            ahead = depth_grad_ref[col + 1, :, at] if col + 1 < cols else zero
            mid = active_ref[col, :, at]
            shifted = (pltpu.roll(mid, 1, 0), mid, pltpu.roll(mid, sub - 1, 0))
            for i in range(3):
                for j, other in enumerate((ahead, here, behind)):
                    totals[3 * i + j] = totals[3 * i + j] + shifted[i] * other
        for t in range(9):
            tap_ref[t : t + 1, at] = jnp.sum(totals[t], axis=0, keepdims=True)
        tap_ref[9:, at] = jnp.zeros((tap_ref.shape[0] - 9, width), F32)


def product_kernel(mine_ref, theirs_ref, depth_ref, other_ref, out_ref):
    dims = (((0,), (0,)), ((), ()))
    out_ref[...] = lax.dot_general(mine_ref[...], depth_ref[...], dims, preferred_element_type=F32) + lax.dot_general(
        theirs_ref[...], other_ref[...], dims, preferred_element_type=F32
    )


def output_kernel(pieces, rows, where_ref, image_ref, grad_ref, proj_ref, norm_ref, depth_grad_ref, one_ref, two_ref, kernel_ref, block_ref, input_ref, halo_ref, flat_ref, flat2_ref):
    cols, sub, channels = image_ref.shape
    even = where_ref[0] % 2 == 0
    has_top = jnp.where(where_ref[0] > 0, 1.0, 0.0)
    has_bottom = jnp.where(where_ref[0] < pieces - 1, 1.0, 0.0)
    line = lax.broadcasted_iota(jnp.int32, (sub, channels), 0)
    one = one_ref[...].astype(F32)
    two = two_ref[...].astype(F32)
    top = jnp.where(even, two, one) * has_top
    bottom = jnp.where(even, one, two) * has_bottom
    center, inverse, gain, shift = (norm_ref[t : t + 1, :] for t in range(4))
    for col in range(cols):
        own = depth_grad_ref[col]
        halo_ref[col] = jnp.where(
            line == rows, bottom[col : col + 1], jnp.where(line == sub - 1, top[col : col + 1], own)
        )
    for start, width in tiles(channels):
        at = pl.ds(start, width)
        taps = [kernel_ref[t : t + 1, at].astype(F32) for t in range(9)]
        before = jnp.zeros((sub, width), F32)
        pending = before
        for col in range(cols):
            mid = halo_ref[col, :, at]
            up = pltpu.roll(mid, 1, 0)
            down = pltpu.roll(mid, sub - 1, 0)
            sums = [taps[j] * down + taps[3 + j] * mid + taps[6 + j] * up for j in range(3)]
            if col:
                last = pending + sums[0]
                image = image_ref[col - 1, :, at]
                halo_ref[col - 1, :, at] = grad_ref[col - 1, :, at] + jnp.where(image > 0, last, 0.0)
            pending = before + sums[1]
            before = sums[2]
        image = image_ref[cols - 1, :, at]
        halo_ref[cols - 1, :, at] = grad_ref[cols - 1, :, at] + jnp.where(image > 0, pending, 0.0)
    for col in range(cols):
        normed = (proj_ref[col * sub : (col + 1) * sub, :] - center) * inverse
        result = image_ref[col] + from_shares(gain * normed + shift, pieces, channels)
        flat_ref[:, col * channels : (col + 1) * channels] = result
        flat2_ref[:, col * channels : (col + 1) * channels] = halo_ref[col]
    block_ref[...] = flat_ref[:rows, :].astype(BF16)
    input_ref[...] = flat2_ref[:rows, :].astype(BF16)


def high_low(values):
    high = values.astype(BF16)
    return high, (values - high.astype(F32)).astype(BF16)


def call(body, outs, *args, smem=(), scratch=()):
    vmem = pl.BlockSpec(memory_space=pltpu.VMEM)
    specs = [pl.BlockSpec(memory_space=pltpu.SMEM) if i in smem else vmem for i in range(len(args))]
    return pl.pallas_call(
        body,
        out_shape=[jax.ShapeDtypeStruct(shape, dtype) for shape, dtype in outs],
        in_specs=specs,
        out_specs=[vmem] * len(outs),
        scratch_shapes=list(scratch),
        compiler_params=pltpu.CompilerParams(vmem_limit_bytes=32 * 1024 * 1024),
    )(*args)


def local(inputs, upstream, labels, class_weights, depth_kernel, point_weight, gain, shift):
    samples, rows, flat = inputs.shape
    assert samples == 1
    channels = point_weight.shape[0]
    cols = flat // channels
    pieces = lax.axis_size("slab")
    copies = lax.axis_size("dp")
    share = channels // pieces
    sub = round_up(rows + 2, SUB)
    padded = round_up(channels, LANES)
    slot = padded // pieces
    me = lax.axis_index("slab")
    where = me.astype(jnp.int32).reshape(1)
    even = me % 2 == 0
    image = inputs.reshape(rows, flat)
    cotangent = upstream.reshape(rows, flat)
    near = [(i, i ^ 1) for i in range(pieces)]
    far = [(i, (i - 1) % pieces if i % 2 == 0 else (i + 1) % pieces) for i in range(pieces)]
    one = lax.ppermute(lax.dynamic_slice_in_dim(image, jnp.where(even, rows - 1, 0), 1, 0), "slab", near)
    two = lax.ppermute(lax.dynamic_slice_in_dim(image, jnp.where(even, 0, rows - 1), 1, 0), "slab", far)

    def prepare(cw, *refs):
        prepare_kernel(pieces, [cw[t] for t in range(3)], *refs)

    lane3 = (cols, sub, channels)
    pixels = cols * sub
    raw, part, grad_out, grad_group, spread_weight = call(
        prepare,
        [(lane3, F32), (lane3, F32), (lane3, F32), ((pixels, padded), F32), ((channels, padded), BF16)],
        class_weights, image, cotangent, labels.reshape(rows, cols), depth_kernel, point_weight,
        smem=(0,),
    )
    depth, projected, active, stats = call(
        lambda *refs: forward_kernel(pieces, *refs, rows),
        [((pixels, channels), BF16), ((pixels, padded), F32), (lane3, F32), ((SUB, padded), F32)],
        where, part, raw, one, two, depth_kernel, spread_weight, grad_group,
        smem=(0,),
        scratch=[pltpu.VMEM(lane3, F32)],
    )
    other_depth = lax.ppermute(depth, "slab", near)
    all_stats = lax.all_gather(stats, "slab", axis=0, tiled=True)
    full, keep, send, norm = call(
        functools.partial(cotangent_kernel, pieces, rows, cols),
        [((pixels, padded), BF16), ((pixels, padded // 2), BF16), ((pixels, padded // 2), BF16), ((SUB, padded), F32)],
        where, all_stats, projected, grad_group, gain.reshape(1, -1), shift.reshape(1, -1),
        smem=(0,),
    )
    theirs = lax.ppermute(send, "slab", near)
    depth_grad, taps, edge_one, edge_two = call(
        functools.partial(backward_kernel, rows),
        [(lane3, F32), ((2 * SUB, channels), F32), ((cols, channels), BF16), ((cols, channels), BF16)],
        full, spread_weight, active, where,
        smem=(3,),
    )
    (blocks,) = call(product_kernel, [((padded // 2, channels), F32)], keep, theirs, depth, other_depth)
    blocks = blocks.reshape(pieces // 2, slot, channels)
    while blocks.shape[0] > 1:
        half = blocks.shape[0] // 2
        high = ((me // 2) & half) != 0
        mine = lax.dynamic_slice_in_dim(blocks, jnp.where(high, half, 0), half, 0)
        other = lax.dynamic_slice_in_dim(blocks, jnp.where(high, 0, half), half, 0).astype(BF16)
        came = lax.ppermute(other, "slab", [(i, i ^ (2 * half)) for i in range(pieces)])
        blocks = mine + came.astype(F32)
    block = blocks[0]
    tap_sum = jnp.sum(lax.all_gather(taps, "slab", axis=0), axis=0)[:9]
    tap_share = lax.dynamic_slice_in_dim(tap_sum, me * share, share, 1)
    place = jnp.where(even, me // 2, pieces // 2 + me // 2) * slot
    group = lax.dynamic_slice_in_dim(norm[4:6], place, share, 1)
    small = jnp.concatenate([tap_share, group], axis=0)
    high, low = high_low(small)
    count = 2 * small.shape[0]
    packed = jnp.concatenate([high, low], axis=0).reshape(-1)
    extra = round_up(count * share, channels) // channels
    packed = jnp.pad(packed, (0, extra * channels - count * share)).reshape(extra, channels)
    total = round_up(share + extra, copies)
    piece = total // copies
    payload = jnp.concatenate([block[:share].astype(BF16), packed], axis=0)
    payload = jnp.pad(payload, ((0, total - payload.shape[0]), (0, 0))).reshape(copies, piece, channels)
    landed = lax.all_to_all(payload, "dp", 0, 0)
    summed = jnp.sum(landed.astype(F32), axis=0)
    gathered = lax.all_to_all(jnp.broadcast_to(summed.astype(BF16)[None], payload.shape), "dp", 0, 0)
    batch = samples * copies
    result = gathered.reshape(total, channels).astype(F32) / batch
    point_out = result[:share].T
    rest = result[share : share + extra].reshape(-1)[: count * share].reshape(2, small.shape[0], share)
    rest = rest[0] + rest[1]

    halo_one = lax.ppermute(edge_one, "slab", near)
    halo_two = lax.ppermute(edge_two, "slab", far)
    block_out, grad_input = call(
        functools.partial(output_kernel, pieces, rows),
        [((rows, flat), BF16), ((rows, flat), BF16)],
        where, raw, grad_out, projected, norm, depth_grad, halo_one, halo_two, depth_kernel,
        smem=(0,),
        scratch=[pltpu.VMEM(lane3, F32), pltpu.VMEM((sub, flat), F32), pltpu.VMEM((sub, flat), F32)],
    )
    return (
        block_out.reshape(inputs.shape),
        grad_input.reshape(inputs.shape),
        point_out,
        rest[:9],
        rest[9],
        rest[10],
    )


def solution(mesh):
    return jax.shard_map(
        local,
        mesh=mesh,
        in_specs=(
            P("dp", "slab", None),
            P("dp", "slab", None),
            P("dp", "slab", None),
            P(),
            P(),
            P(),
            P(),
            P(),
        ),
        out_specs=(
            P("dp", "slab", None),
            P("dp", "slab", None),
            P(None, "slab"),
            P(None, "slab"),
            P("slab"),
            P("slab"),
        ),
        check_vma=False,
    )
```

```python
import functools

import jax
import jax.numpy as jnp
from jax import lax
from jax.experimental import pallas as pl
from jax.experimental.pallas import tpu as pltpu
from jax.sharding import PartitionSpec as P

F32 = jnp.float32
BF16 = jnp.bfloat16
LANES = 128
SUB = 8
EPS = 1e-05
DMA = pltpu.SemaphoreType.DMA


def round_up(value, unit):
    return -(-value // unit) * unit


def tiles(width):
    return [(start, min(LANES, width - start)) for start in range(0, width, LANES)]


def column(ref, col, channels):
    start = col * channels
    base = start // LANES * LANES
    off = start - base
    end = min(ref.shape[1], base + round_up(off + channels, LANES))
    return ref[:, base:end].astype(F32)[:, off : off + channels]


def pixel_weights(class_ref, label_ref):
    labels = label_ref[...]
    weight = jnp.zeros(labels.shape, F32)
    for t in range(class_ref.shape[0]):
        weight = jnp.where(labels == t, class_ref[t], weight)
    return weight


def fetches(sources, buffers, sems):
    copies = [pltpu.make_async_copy(s, b, sems.at[i]) for i, (s, b) in enumerate(zip(sources, buffers))]
    for copy in copies:
        copy.start()
    return copies


def prepare_kernel(class_ref, x_ref, u_ref, label_ref, kernel_ref, active_ref, part_ref, grad_ref, x_buf, u_buf, active_buf, part_buf, sems):
    rows, cols = label_ref.shape
    sub, channels = grad_ref.shape[1:]
    got_x, got_u = fetches((x_ref, u_ref), (x_buf, u_buf), sems)
    put_active = pltpu.make_async_copy(active_buf, active_ref, sems.at[2])
    put_part = pltpu.make_async_copy(part_buf, part_ref, sems.at[3])
    got_x.wait()
    for col in range(cols):
        active_buf[col, :rows, :] = jnp.maximum(column(x_buf, col, channels), 0.0)
        active_buf[col, rows:, :] = jnp.zeros((sub - rows, channels), F32)
    put_active.start()
    for start, width in tiles(channels):
        at = pl.ds(start, width)
        taps = [kernel_ref[t : t + 1, at].astype(F32) for t in range(9)]
        before = jnp.zeros((sub, width), F32)
        pending = before
        for col in range(cols):
            mid = active_buf[col, :, at]
            up = pltpu.roll(mid, 1, 0)
            down = pltpu.roll(mid, sub - 1, 0)
            sums = [taps[j] * up + taps[3 + j] * mid + taps[6 + j] * down for j in range(3)]
            if col:
                part_buf[col - 1, :, at] = pending + sums[2]
            pending = before + sums[1]
            before = sums[0]
        part_buf[cols - 1, :, at] = pending
    put_part.start()
    got_u.wait()
    weight = pixel_weights(class_ref, label_ref)
    for col in range(cols):
        grad_ref[col, :rows, :] = column(u_buf, col, channels) * weight[:, col : col + 1]
        grad_ref[col, rows:, :] = jnp.zeros((sub - rows, channels), F32)
    put_active.wait()
    put_part.wait()


def forward_kernel(pieces, rows, where_ref, part_ref, own_ref, one_ref, two_ref, kernel_ref, point_ref, grad_ref, depth_ref, proj_ref, active_ref, stats_ref, part_buf, active_buf, halo_buf, point_buf, sems):
    cols, sub, channels = part_buf.shape
    got_own, got_part, got_point = fetches((own_ref, part_ref, point_ref), (active_buf, part_buf, point_buf), sems)
    put_active = pltpu.make_async_copy(active_buf, active_ref, sems.at[3])
    even = where_ref[0] % 2 == 0
    has_top = jnp.where(where_ref[0] > 0, 1.0, 0.0)
    has_bottom = jnp.where(where_ref[0] < pieces - 1, 1.0, 0.0)
    line = lax.broadcasted_iota(jnp.int32, (sub, channels), 0)
    wide = [
        jnp.where(line == sub - 1, kernel_ref[j : j + 1, :].astype(F32), kernel_ref[6 + j : 7 + j, :].astype(F32))
        for j in range(3)
    ]
    for col in range(cols):
        one = jnp.maximum(column(one_ref, col, channels), 0.0)
        two = jnp.maximum(column(two_ref, col, channels), 0.0)
        top = jnp.where(even, two, one) * has_top
        bottom = jnp.where(even, one, two) * has_bottom
        halo_buf[col] = jnp.where(line == sub - 1, top, jnp.where(line == rows, bottom, 0.0))
    got_own.wait()
    got_part.wait()
    for start, width in tiles(channels):
        at = pl.ds(start, width)
        row = lax.broadcasted_iota(jnp.int32, (sub, width), 0)
        taps = [w[:, start : start + width] for w in wide]

        def finish(col, value):
            shifted = jnp.where(row == 0, pltpu.roll(value, 1, 0), jnp.where(row == rows - 1, pltpu.roll(value, sub - 1, 0), 0.0))
            total = part_buf[col, :, at] + shifted
            part_buf[col, :, at] = jnp.where(row < rows, total, 0.0)

        before = jnp.zeros((sub, width), F32)
        pending = before
        for col in range(cols):
            halo = halo_buf[col, :, at]
            active_buf[col, :, at] = active_buf[col, :, at] + halo
            if col:
                finish(col - 1, pending + taps[2] * halo)
            pending = before + taps[1] * halo
            before = taps[0] * halo
        finish(cols - 1, pending)
    put_active.start()
    depth = part_buf[...].reshape(cols * sub, channels).astype(BF16)
    depth_ref[:, :channels] = depth
    depth_ref[:, channels:] = jnp.zeros((cols * sub, depth_ref.shape[1] - channels), BF16)
    got_point.wait()
    proj_ref[...] = jnp.dot(depth, point_buf[...], preferred_element_type=F32)
    count = rows * cols
    for start, width in tiles(channels):
        at = pl.ds(start, width)
        proj = proj_ref[:, at]
        grads = grad_ref[:, :, at].reshape(cols * sub, width)
        mine = lax.broadcasted_iota(jnp.int32, (cols * sub, width), 0) % sub < rows
        center = jnp.sum(proj, axis=0, keepdims=True) / count
        deviation = jnp.where(mine, proj - center, 0.0)
        stats_ref[0:1, at] = center
        stats_ref[1:2, at] = jnp.sum(deviation * deviation, axis=0, keepdims=True)
        stats_ref[2:3, at] = jnp.sum(grads, axis=0, keepdims=True)
        stats_ref[3:4, at] = jnp.sum(grads * deviation, axis=0, keepdims=True)
        stats_ref[4:SUB, at] = jnp.zeros((SUB - 4, width), F32)
    put_active.wait()


def cotangent_kernel(pieces, rows, stats_ref, proj_ref, grad_ref, gain_ref, full_ref, norm_ref):
    cols, sub, channels = grad_ref.shape
    local = rows * cols
    count = local * pieces
    stats = [stats_ref[p * SUB : p * SUB + 4, :] for p in range(pieces)]
    center = sum(s[0:1] for s in stats) / pieces
    square = sum(s[1:2] + local * (s[0:1] - center) ** 2 for s in stats)
    shift_part = sum(s[2:3] for s in stats)
    cross = sum(s[3:4] + (s[0:1] - center) * s[2:3] for s in stats)
    inverse = lax.rsqrt(square / count + EPS)
    gain_part = cross * inverse
    gain = gain_ref[...]
    norm_ref[0:1, :] = center
    norm_ref[1:2, :] = inverse
    norm_ref[2:3, :] = gain_part
    norm_ref[3:4, :] = shift_part
    norm_ref[4:SUB, :] = jnp.zeros((SUB - 4, channels), F32)
    for start, width in tiles(channels):
        at = slice(start, start + width)
        mine = lax.broadcasted_iota(jnp.int32, (cols * sub, width), 0) % sub < rows
        normed = (proj_ref[:, start : start + width] - center[:, at]) * inverse[:, at]
        grads = grad_ref[:, :, start : start + width].reshape(cols * sub, width)
        value = (gain * inverse)[:, at] * (grads - (shift_part / count)[:, at] - normed * (gain_part / count)[:, at])
        full_ref[:, start : start + width] = jnp.where(mine, value, 0.0).astype(BF16)
    full_ref[:, channels:] = jnp.zeros((cols * sub, full_ref.shape[1] - channels), BF16)


def product_kernel(pieces, share, where_ref, mine_ref, theirs_ref, depth_ref, other_ref, *refs):
    outs, total_ref = refs[:-1], refs[-1]
    channels = total_ref.shape[1]
    dims = (((0,), (0,)), ((), ()))
    total_ref[...] = lax.dot_general(
        mine_ref[:, :channels], depth_ref[:, :channels], dims, preferred_element_type=F32
    ) + lax.dot_general(theirs_ref[:, :channels], other_ref[:, :channels], dims, preferred_element_type=F32)
    for owner in range(pieces):

        @pl.when(where_ref[0] == owner)
        def _():
            if pieces == 4:
                keep_ref, send_ref = outs
                keep_ref[...] = total_ref[owner * share : (owner + 1) * share, :]
                other = owner ^ 2
                send_ref[...] = total_ref[other * share : (other + 1) * share, :].astype(BF16)
            else:
                for j in range(pieces // 2):
                    place = 2 * j + owner % 2
                    outs[0][j] = total_ref[place * share : (place + 1) * share, :]


def backward_kernel(rows, where_ref, full_ref, point_ref, active_ref, depth_grad_ref, tap_ref, one_ref, two_ref, point_buf, active_buf, grad_buf, sems):
    cols, sub, channels = active_buf.shape
    got_point, got_active = fetches((point_ref, active_ref), (point_buf, active_buf), sems)
    put = pltpu.make_async_copy(grad_buf, depth_grad_ref, sems.at[2])
    got_point.wait()
    grad = lax.dot_general(full_ref[:, :channels], point_buf[...], (((1,), (1,)), ((), ())), preferred_element_type=F32)
    grad_buf[...] = grad.astype(BF16).astype(F32).reshape(cols, sub, channels)
    put.start()
    even = where_ref[0] % 2 == 0
    first = grad_buf[:, 0, :].astype(BF16)
    last = grad_buf[:, rows - 1, :].astype(BF16)
    one_ref[...] = jnp.where(even, last, first)
    two_ref[...] = jnp.where(even, first, last)
    got_active.wait()
    for start, width in tiles(channels):
        at = pl.ds(start, width)
        totals = [jnp.zeros((sub, width), F32) for _ in range(9)]
        zero = jnp.zeros((sub, width), F32)
        ahead = grad_buf[0, :, at]
        here = zero
        for col in range(cols):
            behind, here = here, ahead
            ahead = grad_buf[col + 1, :, at] if col + 1 < cols else zero
            mid = active_buf[col, :, at]
            shifted = (pltpu.roll(mid, 1, 0), mid, pltpu.roll(mid, sub - 1, 0))
            for i in range(3):
                for j, other in enumerate((ahead, here, behind)):
                    totals[3 * i + j] = totals[3 * i + j] + shifted[i] * other
        for t in range(9):
            tap_ref[t : t + 1, at] = jnp.sum(totals[t], axis=0, keepdims=True)
        tap_ref[9:, at] = jnp.zeros((tap_ref.shape[0] - 9, width), F32)
    put.wait()


def pack_kernel(pieces, extra, where_ref, keep_ref, came_ref, taps_ref, norm_ref, out_ref, flat_ref):
    copies, piece, channels = out_ref.shape
    share = keep_ref.shape[0]
    lines = taps_ref.shape[0] // pieces
    taps = sum(taps_ref[p * lines : p * lines + 9, :] for p in range(pieces))
    group = norm_ref[2:4, :]
    small = jnp.concatenate([taps, group], axis=0)
    flat_ref[:share, :] = keep_ref[...] + came_ref[...].astype(F32)
    for owner in range(pieces):

        @pl.when(where_ref[0] == owner)
        def _():
            mine = small[:, owner * share : (owner + 1) * share]
            high = mine.astype(BF16).astype(F32)
            low = mine - high
            spare = extra * pieces - 2 * small.shape[0]
            items = jnp.concatenate([high, low, jnp.zeros((spare, share), F32)], axis=0)
            parts = [items[q * extra : (q + 1) * extra] for q in range(pieces)]
            flat_ref[share : share + extra, :] = jnp.concatenate(parts, axis=1)

    rest = flat_ref.shape[0] - share - extra
    if rest:
        flat_ref[share + extra :, :] = jnp.zeros((rest, channels), F32)
    for k in range(copies):
        out_ref[k] = flat_ref[k * piece : (k + 1) * piece, :].astype(BF16)


def total_kernel(in_ref, out_ref):
    copies = in_ref.shape[0]
    total = in_ref[0].astype(F32)
    for k in range(1, copies):
        total = total + in_ref[k].astype(F32)
    total = total.astype(BF16)
    for k in range(copies):
        out_ref[k] = total


def unpack_kernel(pieces, extra, batch, in_ref, point_ref, tap_ref, gain_ref, shift_ref, flat_ref):
    copies, piece, channels = in_ref.shape
    share = point_ref.shape[0]
    for k in range(copies):
        flat_ref[k * piece : (k + 1) * piece, :] = in_ref[k].astype(F32) / batch
    point_ref[...] = flat_ref[:share, :]
    rest = flat_ref[share : share + extra, :]
    items = jnp.concatenate([rest[:, q * share : (q + 1) * share] for q in range(pieces)], axis=0)
    small = items[:11] + items[11:22]
    tap_ref[...] = small[:9]
    gain_ref[...] = small[9:10]
    shift_ref[...] = small[10:11]


def output_kernel(pieces, rows, where_ref, class_ref, x_ref, u_ref, label_ref, proj_ref, norm_ref, gain_ref, shift_ref, depth_grad_ref, one_ref, two_ref, kernel_ref, block_ref, input_ref, x_buf, u_buf, proj_buf, halo_buf, flat_ref, flat2_ref, sems):
    cols, sub, channels = halo_buf.shape
    got_x, got_proj, got_grad, got_u = fetches((x_ref, proj_ref, depth_grad_ref, u_ref), (x_buf, proj_buf, halo_buf, u_buf), sems)
    even = where_ref[0] % 2 == 0
    has_top = jnp.where(where_ref[0] > 0, 1.0, 0.0)
    has_bottom = jnp.where(where_ref[0] < pieces - 1, 1.0, 0.0)
    center, inverse = norm_ref[0:1, :], norm_ref[1:2, :]
    gain, shift = gain_ref[...], shift_ref[...]
    got_x.wait()
    got_proj.wait()
    for col in range(cols):
        normed = (proj_buf[col * sub : col * sub + rows, :] - center) * inverse
        result = column(x_buf, col, channels) + gain * normed + shift
        flat_ref[:, col * channels : (col + 1) * channels] = result
    block_ref[...] = flat_ref[...].astype(BF16)
    one = one_ref[...].astype(F32)
    two = two_ref[...].astype(F32)
    top = jnp.where(even, two, one) * has_top
    bottom = jnp.where(even, one, two) * has_bottom
    line = lax.broadcasted_iota(jnp.int32, (sub, channels), 0)
    got_grad.wait()
    for col in range(cols):
        halo_buf[col] = jnp.where(
            line == rows, bottom[col : col + 1], jnp.where(line == sub - 1, top[col : col + 1], halo_buf[col])
        )
    for start, width in tiles(channels):
        at = pl.ds(start, width)
        taps = [kernel_ref[t : t + 1, at].astype(F32) for t in range(9)]
        before = jnp.zeros((sub, width), F32)
        pending = before
        for col in range(cols):
            mid = halo_buf[col, :, at]
            up = pltpu.roll(mid, 1, 0)
            down = pltpu.roll(mid, sub - 1, 0)
            sums = [taps[j] * down + taps[3 + j] * mid + taps[6 + j] * up for j in range(3)]
            if col:
                halo_buf[col - 1, :, at] = pending + sums[0]
            pending = before + sums[1]
            before = sums[2]
        halo_buf[cols - 1, :, at] = pending
    got_u.wait()
    weight = pixel_weights(class_ref, label_ref)
    for col in range(cols):
        grads = column(u_buf, col, channels) * weight[:, col : col + 1]
        image = column(x_buf, col, channels)
        flat2_ref[:, col * channels : (col + 1) * channels] = grads + jnp.where(image > 0, halo_buf[col, :rows, :], 0.0)
    input_ref[...] = flat2_ref[...].astype(BF16)


def call(body, ins, outs, scratch=()):
    space = {
        "v": pl.BlockSpec(memory_space=pltpu.VMEM),
        "s": pl.BlockSpec(memory_space=pltpu.SMEM),
        "a": pl.BlockSpec(memory_space=pl.ANY),
    }
    return pl.pallas_call(
        body,
        out_shape=[jax.ShapeDtypeStruct(shape, dtype) for _, shape, dtype in outs],
        in_specs=[space[s] for s, _ in ins],
        out_specs=[space[s] for s, _, _ in outs],
        scratch_shapes=list(scratch),
        compiler_params=pltpu.CompilerParams(vmem_limit_bytes=16 * 1024 * 1024),
    )(*[a for _, a in ins])


def local(inputs, upstream, labels, class_weights, depth_kernel, point_weight, gain, shift):
    samples, rows, flat = inputs.shape
    assert samples == 1
    channels = point_weight.shape[0]
    cols = flat // channels
    pieces = lax.axis_size("slab")
    copies = lax.axis_size("dp")
    assert pieces % 2 == 0
    share = channels // pieces
    sub = round_up(rows + 2, SUB)
    padded = round_up(channels, LANES)
    me = lax.axis_index("slab")
    where = me.astype(jnp.int32).reshape(1)
    even = me % 2 == 0
    image = inputs.reshape(rows, flat)
    cotangent = upstream.reshape(rows, flat)
    label_image = labels.reshape(rows, cols)
    gain, shift = gain.reshape(1, -1), shift.reshape(1, -1)
    near = [(i, i ^ 1) for i in range(pieces)]
    far = [(i, (i - 1) % pieces if i % 2 == 0 else (i + 1) % pieces) for i in range(pieces)]
    lane3 = (cols, sub, channels)
    pixels = cols * sub
    buf3 = pltpu.VMEM(lane3, F32)
    flat_buf = pltpu.VMEM((rows, flat), BF16)
    flat_f32 = pltpu.VMEM((rows, flat), F32)
    point_buf = pltpu.VMEM((channels, channels), BF16)

    two = lax.ppermute(lax.dynamic_slice_in_dim(image, jnp.where(even, 0, rows - 1), 1, 0), "slab", far)
    one = lax.ppermute(lax.dynamic_slice_in_dim(image, jnp.where(even, rows - 1, 0), 1, 0), "slab", near)
    own, part, grad_out = call(
        prepare_kernel,
        [("s", class_weights), ("a", image), ("a", cotangent), ("v", label_image), ("v", depth_kernel)],
        [("a", lane3, F32), ("a", lane3, F32), ("v", lane3, F32)],
        [flat_buf, flat_buf, buf3, buf3, DMA((4,))],
    )
    depth, projected, active, stats = call(
        functools.partial(forward_kernel, pieces, rows),
        [("s", where), ("a", part), ("a", own), ("v", one), ("v", two), ("v", depth_kernel), ("a", point_weight), ("v", grad_out)],
        [("v", (pixels, padded), BF16), ("v", (pixels, channels), F32), ("a", lane3, F32), ("v", (SUB, channels), F32)],
        [buf3, buf3, buf3, point_buf, DMA((4,))],
    )
    other_depth = lax.ppermute(depth, "slab", near)
    all_stats = lax.all_gather(stats, "slab", axis=0, tiled=True)
    full, norm = call(
        functools.partial(cotangent_kernel, pieces, rows),
        [("v", all_stats), ("v", projected), ("v", grad_out), ("v", gain)],
        [("v", (pixels, padded), BF16), ("v", (SUB, channels), F32)],
    )
    theirs = lax.ppermute(full, "slab", near)
    product_outs = (
        [("v", (share, channels), F32), ("v", (share, channels), BF16)]
        if pieces == 4
        else [("v", (pieces // 2, share, channels), F32)]
    )
    products = call(
        functools.partial(product_kernel, pieces, share),
        [("s", where), ("v", full), ("v", theirs), ("v", depth), ("v", other_depth)],
        product_outs,
        [pltpu.VMEM((channels, channels), F32)],
    )
    if pieces == 4:
        keep, leaving = products
    else:
        blocks = products[0]
        while blocks.shape[0] > 2:
            half = blocks.shape[0] // 2
            high = ((me // 2) & half) != 0
            mine = lax.dynamic_slice_in_dim(blocks, jnp.where(high, half, 0), half, 0)
            leaving = lax.dynamic_slice_in_dim(blocks, jnp.where(high, 0, half), half, 0).astype(BF16)
            blocks = mine + lax.ppermute(leaving, "slab", [(i, i ^ (2 * half)) for i in range(pieces)]).astype(F32)
        if pieces == 2:
            keep, leaving = blocks[0], jnp.zeros((share, channels), BF16)
        else:
            keep = lax.dynamic_index_in_dim(blocks, (me // 2) % 2, 0, False)
            leaving = lax.dynamic_index_in_dim(blocks, 1 - (me // 2) % 2, 0, False).astype(BF16)
    leaving, full = lax.optimization_barrier((leaving, full))
    came = lax.ppermute(leaving, "slab", [(i, i ^ 2) for i in range(pieces)]) if pieces > 2 else leaving
    depth_grad, taps, edge_one, edge_two = call(
        functools.partial(backward_kernel, rows),
        [("s", where), ("v", full), ("a", point_weight), ("a", active)],
        [("a", lane3, F32), ("v", (2 * SUB, channels), F32), ("v", (cols, channels), BF16), ("v", (cols, channels), BF16)],
        [point_buf, buf3, buf3, DMA((3,))],
    )
    all_taps = lax.all_gather(taps, "slab", axis=0, tiled=True)
    extra = -(-22 // pieces)
    piece = -(-(share + extra) // copies)
    total = piece * copies
    payload = (copies, piece, channels)
    batch = samples * copies
    (packed,) = call(
        functools.partial(pack_kernel, pieces, extra),
        [("s", where), ("v", keep), ("v", came), ("v", all_taps), ("v", norm)],
        [("v", payload, BF16)],
        [pltpu.VMEM((total, channels), F32)],
    )
    landed = lax.all_to_all(packed, "dp", 0, 0)
    (summed,) = call(total_kernel, [("v", landed)], [("v", payload, BF16)])
    gathered = lax.all_to_all(summed, "dp", 0, 0)
    halo_one = lax.ppermute(edge_one, "slab", near)
    halo_two = lax.ppermute(edge_two, "slab", far)
    block_out, grad_input = call(
        functools.partial(output_kernel, pieces, rows),
        [("s", where), ("s", class_weights), ("a", image), ("a", cotangent), ("v", label_image), ("a", projected), ("v", norm), ("v", gain), ("v", shift), ("a", depth_grad), ("v", halo_one), ("v", halo_two), ("v", depth_kernel)],
        [("v", (rows, flat), BF16), ("v", (rows, flat), BF16)],
        [flat_buf, flat_buf, pltpu.VMEM((pixels, channels), F32), buf3, flat_f32, flat_f32, DMA((4,))],
    )
    point_out, tap_out, gain_out, shift_out = call(
        functools.partial(unpack_kernel, pieces, extra, batch),
        [("v", gathered)],
        [("v", (share, channels), F32), ("v", (9, share), F32), ("v", (1, share), F32), ("v", (1, share), F32)],
        [pltpu.VMEM((total, channels), F32)],
    )
    return (
        block_out.reshape(inputs.shape),
        grad_input.reshape(inputs.shape),
        point_out.T,
        tap_out,
        gain_out[0],
        shift_out[0],
    )


def solution(mesh):
    return jax.shard_map(
        local,
        mesh=mesh,
        in_specs=(
            P("dp", "slab", None),
            P("dp", "slab", None),
            P("dp", "slab", None),
            P(),
            P(),
            P(),
            P(),
            P(),
        ),
        out_specs=(
            P("dp", "slab", None),
            P("dp", "slab", None),
            P(None, "slab"),
            P(None, "slab"),
            P("slab"),
            P("slab"),
        ),
        check_vma=False,
    )
```

```python
import functools

import jax
import jax.numpy as jnp
from jax import lax
from jax.experimental import pallas as pl
from jax.experimental.pallas import tpu as pltpu
from jax.sharding import PartitionSpec as P

F32 = jnp.float32
BF16 = jnp.bfloat16
LANES = 128
SUB = 8
EPS = 1e-05
DMA = pltpu.SemaphoreType.DMA


def round_up(value, unit):
    return -(-value // unit) * unit


def tiles(width):
    return [(start, min(LANES, width - start)) for start in range(0, width, LANES)]


def column(ref, col, channels):
    start = col * channels
    base = start // LANES * LANES
    off = start - base
    end = min(ref.shape[1], base + round_up(off + channels, LANES))
    return ref[:, base:end].astype(F32)[:, off : off + channels]


def pixel_weights(class_ref, label_ref):
    labels = jnp.concatenate([label_ref[r] for r in range(label_ref.shape[0])], axis=0)
    weight = jnp.zeros(labels.shape, F32)
    for t in range(class_ref.shape[0]):
        weight = jnp.where(labels == t, class_ref[t], weight)
    return weight


def fetches(sources, buffers, sems):
    copies = [pltpu.make_async_copy(s, b, sems.at[i]) for i, (s, b) in enumerate(zip(sources, buffers))]
    for copy in copies:
        copy.start()
    return copies


def prepare_kernel(class_ref, x_ref, u_ref, label_ref, kernel_ref, active_ref, part_ref, grad_ref, class_buf, x_buf, u_buf, label_buf, kernel_buf, sems):
    rows, _, cols = label_buf.shape
    sub, channels = grad_ref.shape[1:]
    got_x, got_kernel, got_u, got_label, got_class = fetches(
        (x_ref.at[0], kernel_ref, u_ref.at[0], label_ref, class_ref), (x_buf, kernel_buf, u_buf, label_buf, class_buf), sems
    )
    got_x.wait()
    for col in range(cols):
        active_ref[col, :rows, :] = jnp.maximum(column(x_buf, col, channels), 0.0)
        active_ref[col, rows:, :] = jnp.zeros((sub - rows, channels), F32)
    got_kernel.wait()
    for start, width in tiles(channels):
        at = pl.ds(start, width)
        taps = [kernel_buf[t : t + 1, at].astype(F32) for t in range(9)]
        before = jnp.zeros((sub, width), F32)
        pending = before
        for col in range(cols):
            mid = active_ref[col, :, at]
            up = pltpu.roll(mid, 1, 0)
            down = pltpu.roll(mid, sub - 1, 0)
            sums = [taps[j] * up + taps[3 + j] * mid + taps[6 + j] * down for j in range(3)]
            if col:
                part_ref[col - 1, :, at] = pending + sums[2]
            pending = before + sums[1]
            before = sums[0]
        part_ref[cols - 1, :, at] = pending
    got_u.wait()
    got_label.wait()
    got_class.wait()
    weight = pixel_weights(class_buf, label_buf)
    for col in range(cols):
        grad_ref[col, :rows, :] = column(u_buf, col, channels) * weight[:, col : col + 1]
        grad_ref[col, rows:, :] = jnp.zeros((sub - rows, channels), F32)


def forward_kernel(pieces, rows, where_ref, part_ref, own_ref, one_ref, two_ref, kernel_ref, point_ref, grad_ref, depth_ref, proj_ref, active_ref, stats_ref, part_buf, active_buf, halo_buf, point_buf, kernel_buf, sems):
    cols, sub, channels = part_buf.shape
    got_kernel, got_point = fetches((kernel_ref, point_ref), (kernel_buf, point_buf), sems)
    put_active = pltpu.make_async_copy(active_buf, active_ref, sems.at[2])
    even = where_ref[0] % 2 == 0
    has_top = jnp.where(where_ref[0] > 0, 1.0, 0.0)
    has_bottom = jnp.where(where_ref[0] < pieces - 1, 1.0, 0.0)
    for col in range(cols):
        start = col * channels
        base = start // LANES * LANES
        off = start - base
        end = min(two_ref.shape[1], base + round_up(off + channels, LANES))
        near = one_ref[0, :, base:end].astype(F32)
        one = jnp.maximum(jnp.where(even, near[:1], near[rows - 1 :]), 0.0)
        two = jnp.maximum(two_ref[:, base:end].astype(F32), 0.0)
        top = jnp.where(even, two, one) * has_top
        bottom = jnp.where(even, one, two) * has_bottom
        line = lax.broadcasted_iota(jnp.int32, (sub, end - base), 0)
        lines = jnp.where(line == sub - 1, top, jnp.where(line == rows, bottom, 0.0))
        halo_buf[col] = lines[:, off : off + channels]
    got_kernel.wait()
    line = lax.broadcasted_iota(jnp.int32, (sub, channels), 0)
    wide = [
        jnp.where(line == sub - 1, kernel_buf[j : j + 1, :].astype(F32), kernel_buf[6 + j : 7 + j, :].astype(F32))
        for j in range(3)
    ]
    for start, width in tiles(channels):
        at = pl.ds(start, width)
        row = lax.broadcasted_iota(jnp.int32, (sub, width), 0)
        taps = [w[:, start : start + width] for w in wide]

        def finish(col, value):
            shifted = jnp.where(row == 0, pltpu.roll(value, 1, 0), jnp.where(row == rows - 1, pltpu.roll(value, sub - 1, 0), 0.0))
            total = part_ref[col, :, at] + shifted
            part_buf[col, :, at] = jnp.where(row < rows, total, 0.0)

        before = jnp.zeros((sub, width), F32)
        pending = before
        for col in range(cols):
            halo = halo_buf[col, :, at]
            active_buf[col, :, at] = own_ref[col, :, at] + halo
            if col:
                finish(col - 1, pending + taps[2] * halo)
            pending = before + taps[1] * halo
            before = taps[0] * halo
        finish(cols - 1, pending)
    put_active.start()
    depth = part_buf[...].reshape(cols * sub, channels).astype(BF16)
    depth_ref[:, :channels] = depth
    depth_ref[:, channels:] = jnp.zeros((cols * sub, depth_ref.shape[1] - channels), BF16)
    got_point.wait()
    proj_ref[...] = jnp.dot(depth, point_buf[...], preferred_element_type=F32)
    count = rows * cols
    for start, width in tiles(channels):
        at = pl.ds(start, width)
        proj = proj_ref[:, at]
        grads = grad_ref[:, :, at].reshape(cols * sub, width)
        mine = lax.broadcasted_iota(jnp.int32, (cols * sub, width), 0) % sub < rows
        center = jnp.sum(proj, axis=0, keepdims=True) / count
        deviation = jnp.where(mine, proj - center, 0.0)
        stats_ref[0:1, at] = center
        stats_ref[1:2, at] = jnp.sum(deviation * deviation, axis=0, keepdims=True)
        stats_ref[2:3, at] = jnp.sum(grads, axis=0, keepdims=True)
        stats_ref[3:4, at] = jnp.sum(grads * deviation, axis=0, keepdims=True)
        stats_ref[4:SUB, at] = jnp.zeros((SUB - 4, width), F32)
    put_active.wait()


def paired_sum(values):
    while len(values) > 1:
        values = [sum(values[i : i + 2]) for i in range(0, len(values), 2)]
    return values[0]


def cotangent_kernel(pieces, rows, proj_ref, grad_ref, gain_ref, _, *refs):
    stats_refs, (full_ref, norm_ref) = refs[:-2], refs[-2:]
    cols, sub, channels = grad_ref.shape
    local = rows * cols
    count = local * pieces
    stats = [ref[p : p + 4, :] for ref in stats_refs for p in range(0, ref.shape[0], SUB)]
    center = paired_sum([s[0:1] for s in stats]) / pieces
    square = paired_sum([s[1:2] + local * (s[0:1] - center) ** 2 for s in stats])
    shift_part = paired_sum([s[2:3] for s in stats])
    cross = paired_sum([s[3:4] + (s[0:1] - center) * s[2:3] for s in stats])
    inverse = lax.rsqrt(square / count + EPS)
    gain_part = cross * inverse
    gain = gain_ref[...].reshape(1, channels)
    norm_ref[0:1, :] = center
    norm_ref[1:2, :] = inverse
    norm_ref[2:3, :] = gain_part
    norm_ref[3:4, :] = shift_part
    norm_ref[4:SUB, :] = jnp.zeros((SUB - 4, channels), F32)
    for start, width in tiles(channels):
        at = slice(start, start + width)
        mine = lax.broadcasted_iota(jnp.int32, (cols * sub, width), 0) % sub < rows
        normed = (proj_ref[:, start : start + width] - center[:, at]) * inverse[:, at]
        grads = grad_ref[:, :, start : start + width].reshape(cols * sub, width)
        value = (gain * inverse)[:, at] * (grads - (shift_part / count)[:, at] - normed * (gain_part / count)[:, at])
        full_ref[:, start : start + width] = jnp.where(mine, value, 0.0).astype(BF16)
    full_ref[:, channels:] = jnp.zeros((cols * sub, full_ref.shape[1] - channels), BF16)


def product_kernel(full_ref, depth_ref, out_ref):
    channels = out_ref.shape[1]
    out_ref[...] = lax.dot_general(
        full_ref[:, :channels], depth_ref[:, :channels], (((0,), (0,)), ((), ())), preferred_element_type=F32
    )


def shares_kernel(pieces, share, where_ref, full_ref, depth_ref, own_ref, *refs):
    outs, total_ref = refs[:-1], refs[-1]
    product_kernel(full_ref, depth_ref, total_ref)
    for owner in range(pieces):

        @pl.when(where_ref[0] == owner)
        def _():
            def part(place):
                at = slice(place * share, (place + 1) * share)
                return total_ref[at, :] + own_ref[at, :]

            if pieces == 4:
                keep_ref, send_ref = outs
                keep_ref[...] = part(owner)
                send_ref[...] = part(owner ^ 2).astype(BF16)
            else:
                for j in range(pieces // 2):
                    outs[0][j] = part(2 * j + owner % 2)


def backward_kernel(rows, where_ref, full_ref, point_ref, active_ref, depth_grad_ref, tap_ref, one_ref, two_ref, point_buf, active_buf, grad_buf, sems):
    cols, sub, channels = active_buf.shape
    got_point, got_active = fetches((point_ref, active_ref), (point_buf, active_buf), sems)
    put = pltpu.make_async_copy(grad_buf, depth_grad_ref, sems.at[2])
    got_point.wait()
    grad = lax.dot_general(full_ref[:, :channels], point_buf[...], (((1,), (1,)), ((), ())), preferred_element_type=F32)
    grad_buf[...] = grad.astype(BF16).astype(F32).reshape(cols, sub, channels)
    put.start()
    even = where_ref[0] % 2 == 0
    first = grad_buf[:, 0, :].astype(BF16)
    last = grad_buf[:, rows - 1, :].astype(BF16)
    one_ref[...] = jnp.where(even, last, first)
    two_ref[...] = jnp.where(even, first, last)
    got_active.wait()
    for start, width in tiles(channels):
        at = pl.ds(start, width)
        totals = [jnp.zeros((sub, width), F32) for _ in range(9)]
        zero = jnp.zeros((sub, width), F32)
        ahead = grad_buf[0, :, at]
        here = zero
        for col in range(cols):
            behind, here = here, ahead
            ahead = grad_buf[col + 1, :, at] if col + 1 < cols else zero
            mid = active_buf[col, :, at]
            shifted = (pltpu.roll(mid, 1, 0), mid, pltpu.roll(mid, sub - 1, 0))
            for i in range(3):
                for j, other in enumerate((ahead, here, behind)):
                    totals[3 * i + j] = totals[3 * i + j] + shifted[i] * other
        for t in range(9):
            tap_ref[t : t + 1, at] = jnp.sum(totals[t], axis=0, keepdims=True)
        tap_ref[9:, at] = jnp.zeros((tap_ref.shape[0] - 9, width), F32)
    put.wait()


def fold(small, pieces, owner):
    share = small.shape[1] // pieces
    lines = -(-small.shape[0] // pieces)
    mine = small[:, owner * share : (owner + 1) * share]
    spare = lines * pieces - small.shape[0]
    if spare:
        mine = jnp.concatenate([mine, jnp.zeros((spare, share), F32)], axis=0)
    return jnp.concatenate([mine[q * lines : (q + 1) * lines] for q in range(pieces)], axis=1)


def unfold(lines, pieces, count):
    share = lines.shape[1] // pieces
    return jnp.concatenate([lines[:, q * share : (q + 1) * share] for q in range(pieces)], axis=0)[:count]


def store_halves(ref, start, lines):
    count = lines.shape[0]
    high = lines.astype(BF16).astype(F32)
    ref[start : start + count, :] = high
    ref[start + count : start + 2 * count, :] = lines - high


def small_kernel(pieces, where_ref, taps_ref, other_ref, norm_ref, stay_ref, leave_ref):
    taps = taps_ref[:9, :] + other_ref[:9, :]
    group = norm_ref[2:4, :]
    stay = jnp.concatenate([taps, group], axis=0)
    leave = jnp.concatenate([taps, jnp.zeros_like(group)], axis=0)
    for owner in range(pieces):

        @pl.when(where_ref[0] == owner)
        def _():
            stay_ref[...] = fold(stay, pieces, owner)
            leave_ref[...] = fold(leave, pieces, owner ^ 2)


def fold_kernel(pieces, where_ref, taps_ref, norm_ref, stay_ref, leave_ref):
    step = taps_ref.shape[0] // pieces
    taps = sum(taps_ref[p * step : p * step + 9, :] for p in range(pieces))
    small = jnp.concatenate([taps, norm_ref[2:4, :]], axis=0)
    for owner in range(pieces):

        @pl.when(where_ref[0] == owner)
        def _():
            stay_ref[...] = fold(small, pieces, owner)

    leave_ref[...] = jnp.zeros(leave_ref.shape, F32)


def pack_kernel(keep_ref, came_ref, fold_ref, other_ref, out_ref, flat_ref):
    copies, piece, channels = out_ref.shape
    share, lines = keep_ref.shape[0], fold_ref.shape[0]
    flat_ref[:share, :] = keep_ref[...] + came_ref[...].astype(F32)
    store_halves(flat_ref, share, fold_ref[...] + other_ref[...])
    rest = flat_ref.shape[0] - share - 2 * lines
    if rest:
        flat_ref[share + 2 * lines :, :] = jnp.zeros((rest, channels), F32)
    for k in range(copies):
        out_ref[k] = flat_ref[k * piece : (k + 1) * piece, :].astype(BF16)


def total_kernel(in_ref, out_ref):
    copies = in_ref.shape[0]
    total = in_ref[0].astype(F32)
    for k in range(1, copies):
        total = total + in_ref[k].astype(F32)
    total = total.astype(BF16)
    for k in range(copies):
        out_ref[k] = total


def unpack_kernel(pieces, batch, *refs):
    ins, (point_ref, tap_ref, gain_ref, shift_ref, flat_ref) = refs[:-5], refs[-5:]
    share = point_ref.shape[0]
    start = 0
    for in_ref in ins:
        copies, piece, _ = in_ref.shape
        for k in range(copies):
            flat_ref[start : start + piece, :] = in_ref[k].astype(F32) / batch
            start += piece
    point_ref[...] = flat_ref[:share, :]
    lines = -(-11 // pieces)
    total = flat_ref[share : share + lines, :] + flat_ref[share + lines : share + 2 * lines, :]
    small = unfold(total, pieces, 11)
    tap_ref[...] = small[:9]
    gain_ref[...] = small[9:10].reshape(share)
    shift_ref[...] = small[10:11].reshape(share)


def output_kernel(pieces, rows, where_ref, class_ref, x_ref, u_ref, label_ref, proj_ref, norm_ref, gain_ref, shift_ref, depth_grad_ref, one_ref, two_ref, kernel_ref, block_ref, input_ref, x_buf, u_buf, proj_buf, halo_buf, flat_ref, flat2_ref, class_buf, label_buf, kernel_buf, sems):
    cols, sub, channels = halo_buf.shape
    got_x, got_proj, got_grad, got_kernel, got_u, got_label, got_class = fetches(
        (x_ref.at[0], proj_ref, depth_grad_ref, kernel_ref, u_ref.at[0], label_ref, class_ref),
        (x_buf, proj_buf, halo_buf, kernel_buf, u_buf, label_buf, class_buf),
        sems,
    )
    even = where_ref[0] % 2 == 0
    has_top = jnp.where(where_ref[0] > 0, 1.0, 0.0)
    has_bottom = jnp.where(where_ref[0] < pieces - 1, 1.0, 0.0)
    center, inverse = norm_ref[0:1, :], norm_ref[1:2, :]
    gain, shift = gain_ref[...].reshape(1, channels), shift_ref[...].reshape(1, channels)
    got_x.wait()
    got_proj.wait()
    for col in range(cols):
        normed = (proj_buf[col * sub : col * sub + rows, :] - center) * inverse
        result = column(x_buf, col, channels) + gain * normed + shift
        flat_ref[:, col * channels : (col + 1) * channels] = result
    block_ref[...] = flat_ref[...].astype(BF16)
    one = one_ref[...].astype(F32)
    two = two_ref[...].astype(F32)
    top = jnp.where(even, two, one) * has_top
    bottom = jnp.where(even, one, two) * has_bottom
    line = lax.broadcasted_iota(jnp.int32, (sub, channels), 0)
    got_grad.wait()
    got_kernel.wait()
    for col in range(cols):
        halo_buf[col] = jnp.where(
            line == rows, bottom[col : col + 1], jnp.where(line == sub - 1, top[col : col + 1], halo_buf[col])
        )
    for start, width in tiles(channels):
        at = pl.ds(start, width)
        taps = [kernel_buf[t : t + 1, at].astype(F32) for t in range(9)]
        before = jnp.zeros((sub, width), F32)
        pending = before
        for col in range(cols):
            mid = halo_buf[col, :, at]
            up = pltpu.roll(mid, 1, 0)
            down = pltpu.roll(mid, sub - 1, 0)
            sums = [taps[j] * down + taps[3 + j] * mid + taps[6 + j] * up for j in range(3)]
            if col:
                halo_buf[col - 1, :, at] = pending + sums[0]
            pending = before + sums[1]
            before = sums[2]
        halo_buf[cols - 1, :, at] = pending
    got_u.wait()
    got_label.wait()
    got_class.wait()
    weight = pixel_weights(class_buf, label_buf)
    for col in range(cols):
        grads = column(u_buf, col, channels) * weight[:, col : col + 1]
        image = column(x_buf, col, channels)
        flat2_ref[:, col * channels : (col + 1) * channels] = grads + jnp.where(image > 0, halo_buf[col, :rows, :], 0.0)
    input_ref[...] = flat2_ref[...].astype(BF16)


def call(body, ins, outs, scratch=(), megabytes=16):
    space = {
        "o": pl.BlockSpec(memory_space=pl.ANY),
        "v": pl.BlockSpec(memory_space=pltpu.VMEM),
        "s": pl.BlockSpec(memory_space=pltpu.SMEM),
        "a": pl.BlockSpec(memory_space=pl.ANY),
    }
    return pl.pallas_call(
        body,
        out_shape=[jax.ShapeDtypeStruct(shape, dtype) for _, shape, dtype in outs],
        in_specs=[space[s] for s, _ in ins],
        out_specs=[space[s] for s, _, _ in outs],
        scratch_shapes=list(scratch),
        compiler_params=pltpu.CompilerParams(vmem_limit_bytes=megabytes * 1024 * 1024),
    )(*[pltpu.with_memory_space_constraint(a, pltpu.HBM) if s == "a" else a for s, a in ins])


def local(inputs, upstream, labels, class_weights, depth_kernel, point_weight, gain, shift):
    samples, rows, flat = inputs.shape
    assert samples == 1
    channels = point_weight.shape[0]
    cols = flat // channels
    pieces = lax.axis_size("slab")
    copies = lax.axis_size("dp")
    assert pieces % 2 == 0
    share = channels // pieces
    sub = round_up(rows + 2, SUB)
    padded = round_up(channels, LANES)
    me = lax.axis_index("slab")
    where = me.astype(jnp.int32).reshape(1)
    even = me % 2 == 0
    image = inputs.reshape(rows, flat)
    near = [(i, i ^ 1) for i in range(pieces)]
    far = [(i, (i - 1) % pieces if i % 2 == 0 else (i + 1) % pieces) for i in range(pieces)]
    lane3 = (cols, sub, channels)
    pixels = cols * sub
    buf3 = pltpu.VMEM(lane3, F32)
    flat_buf = pltpu.VMEM((rows, flat), BF16)
    flat_f32 = pltpu.VMEM((rows, flat), F32)
    point_buf = pltpu.VMEM((channels, channels), BF16)
    kernel_buf = pltpu.VMEM(depth_kernel.shape, BF16)
    label_buf = pltpu.VMEM((rows, 1, cols), labels.dtype)
    label_lines = jnp.transpose(labels, (1, 0, 2))
    class_buf = pltpu.SMEM(class_weights.shape, F32)

    one = lax.ppermute(inputs, "slab", near)
    two = lax.ppermute(lax.dynamic_slice_in_dim(image, jnp.where(even, 0, rows - 1), 1, 0), "slab", far)
    own, part, grad_out = call(
        prepare_kernel,
        [("a", class_weights), ("a", inputs), ("a", upstream), ("a", label_lines), ("a", depth_kernel)],
        [("v", lane3, F32), ("v", lane3, F32), ("v", lane3, F32)],
        [class_buf, flat_buf, flat_buf, label_buf, kernel_buf, DMA((5,))],
        megabytes=16,
    )
    depth, projected, active, stats = call(
        functools.partial(forward_kernel, pieces, rows),
        [("s", where), ("v", part), ("v", own), ("v", one), ("v", two), ("a", depth_kernel), ("a", point_weight), ("v", grad_out)],
        [("v", (pixels, padded), BF16), ("v", (pixels, channels), F32), ("a", lane3, F32), ("v", (SUB, channels), F32)],
        [buf3, buf3, buf3, point_buf, kernel_buf, DMA((3,))],
    )
    other_depth = lax.ppermute(depth, "slab", near)
    across = [(i, i ^ 2) for i in range(pieces)]
    if pieces == 4:
        apart = [(i, i ^ 3) for i in range(pieces)]
        all_stats = [stats, *(lax.ppermute(stats, "slab", pairs) for pairs in (near, across, apart))]
    else:
        all_stats = [lax.all_gather(stats, "slab", axis=0, tiled=True)]
    full, norm = call(
        functools.partial(cotangent_kernel, pieces, rows),
        [("v", projected), ("v", grad_out), ("v", gain), ("o", other_depth), *(("v", part) for part in all_stats)],
        [("v", (pixels, padded), BF16), ("v", (SUB, channels), F32)],
    )
    theirs = lax.ppermute(full, "slab", near)
    (own_product,) = call(product_kernel, [("v", full), ("v", depth)], [("v", (channels, channels), F32)])
    lines = -(-11 // pieces)
    batch = samples * copies
    if pieces == 4:
        share_outs = [("v", (share, channels), F32), ("v", (share, channels), BF16)]
    else:
        share_outs = [("v", (pieces // 2, share, channels), F32)]
    products = call(
        functools.partial(shares_kernel, pieces, share),
        [("s", where), ("v", theirs), ("v", other_depth), ("v", own_product)],
        share_outs,
        [pltpu.VMEM((channels, channels), F32)],
    )
    if pieces == 4:
        keep, leaving = products
    else:
        blocks = products[0]
        while blocks.shape[0] > 2:
            half = blocks.shape[0] // 2
            high = ((me // 2) & half) != 0
            mine = lax.dynamic_slice_in_dim(blocks, jnp.where(high, half, 0), half, 0)
            leaving = lax.dynamic_slice_in_dim(blocks, jnp.where(high, 0, half), half, 0).astype(BF16)
            came = lax.ppermute(leaving, "slab", [(i, i ^ (2 * half)) for i in range(pieces)])
            blocks = mine + came.astype(F32)
        bit = (me // 2) % 2
        keep = blocks[0] if pieces == 2 else lax.dynamic_index_in_dim(blocks, bit, 0, False)
        leaving = None if pieces == 2 else lax.dynamic_index_in_dim(blocks, 1 - bit, 0, False).astype(BF16)
    if pieces > 2:
        leaving, full = lax.optimization_barrier((leaving, full))
        came = lax.ppermute(leaving, "slab", across)
    else:
        came = jnp.zeros((share, channels), BF16)
    depth_grad, taps, edge_one, edge_two = call(
        functools.partial(backward_kernel, rows),
        [("s", where), ("v", full), ("o", point_weight), ("o", active)],
        [("a", lane3, F32), ("v", (2 * SUB, channels), F32), ("v", (cols, channels), BF16), ("v", (cols, channels), BF16)],
        [point_buf, buf3, buf3, DMA((3,))],
    )
    fold_outs = [("v", (lines, channels), F32)] * 2
    if pieces == 4:
        stay, leave = call(
            functools.partial(small_kernel, pieces),
            [("s", where), ("v", taps), ("v", lax.ppermute(taps, "slab", near)), ("v", norm)],
            fold_outs,
        )
        leave = lax.ppermute(leave, "slab", across)
    else:
        all_taps = lax.all_gather(taps, "slab", axis=0, tiled=True)
        stay, leave = call(functools.partial(fold_kernel, pieces), [("s", where), ("v", all_taps), ("v", norm)], fold_outs)
    piece = -(-(share + 2 * lines) // copies)
    total = piece * copies
    (packed,) = call(
        pack_kernel,
        [("v", keep), ("v", came), ("v", stay), ("v", leave)],
        [("v", (copies, piece, channels), BF16)],
        [pltpu.VMEM((total, channels), F32)],
    )
    landed = lax.all_to_all(packed, "dp", 0, 0)
    (summed,) = call(total_kernel, [("v", landed)], [("v", packed.shape, BF16)])
    gathered = lax.all_to_all(summed, "dp", 0, 0)
    halo_one = lax.ppermute(edge_one, "slab", near)
    halo_two = lax.ppermute(edge_two, "slab", far)
    block_out, grad_input = call(
        functools.partial(output_kernel, pieces, rows),
        [("s", where), ("a", class_weights), ("a", inputs), ("a", upstream), ("a", label_lines), ("a", projected), ("v", norm), ("v", gain), ("v", shift), ("a", depth_grad), ("v", halo_one), ("v", halo_two), ("a", depth_kernel)],
        [("v", (rows, flat), BF16), ("v", (rows, flat), BF16)],
        [flat_buf, flat_buf, pltpu.VMEM((pixels, channels), F32), buf3, flat_f32, flat_f32, class_buf, label_buf, kernel_buf, DMA((7,))],
        megabytes=16,
    )
    point_out, tap_out, gain_out, shift_out = call(
        functools.partial(unpack_kernel, pieces, batch),
        [("v", gathered)],
        [("v", (share, channels), F32), ("v", (9, share), F32), ("v", (share,), F32), ("v", (share,), F32)],
        [pltpu.VMEM((total, channels), F32)],
    )
    return (
        block_out.reshape(inputs.shape),
        grad_input.reshape(inputs.shape),
        point_out.T,
        tap_out,
        gain_out,
        shift_out,
    )


def solution(mesh):
    return jax.shard_map(
        local,
        mesh=mesh,
        in_specs=(
            P("dp", "slab", None),
            P("dp", "slab", None),
            P("dp", "slab", None),
            P(),
            P(),
            P(),
            P(),
            P(),
        ),
        out_specs=(
            P("dp", "slab", None),
            P("dp", "slab", None),
            P(None, "slab"),
            P(None, "slab"),
            P("slab"),
            P("slab"),
        ),
        check_vma=False,
    )
```

```python
import functools

import jax
import jax.numpy as jnp
from jax import lax
from jax.experimental import pallas as pl
from jax.experimental.pallas import tpu as pltpu
from jax.sharding import PartitionSpec as P

F32 = jnp.float32
BF16 = jnp.bfloat16
LANES = 128
SUB = 8
EPS = 1e-05
DMA = pltpu.SemaphoreType.DMA


def round_up(value, unit):
    return -(-value // unit) * unit


def tiles(width):
    return [(start, min(LANES, width - start)) for start in range(0, width, LANES)]


def column(ref, col, channels):
    start = col * channels
    base = start // LANES * LANES
    off = start - base
    end = min(ref.shape[1], base + round_up(off + channels, LANES))
    return ref[:, base:end].astype(F32)[:, off : off + channels]


def pixel_weights(class_ref, label_ref):
    labels = jnp.concatenate([label_ref[r] for r in range(label_ref.shape[0])], axis=0)
    weight = jnp.zeros(labels.shape, F32)
    for t in range(class_ref.shape[0]):
        weight = jnp.where(labels == t, class_ref[t], weight)
    return weight


def fetches(sources, buffers, sems):
    copies = [pltpu.make_async_copy(s, b, sems.at[i]) for i, (s, b) in enumerate(zip(sources, buffers))]
    for copy in copies:
        copy.start()
    return copies


def prepare_kernel(class_ref, x_ref, u_ref, label_ref, kernel_ref, active_ref, part_ref, grad_ref, class_buf, x_buf, u_buf, label_buf, kernel_buf, sems):
    rows, _, cols = label_buf.shape
    sub, channels = grad_ref.shape[1:]
    got_x, got_kernel, got_u, got_label, got_class = fetches(
        (x_ref.at[0], kernel_ref, u_ref.at[0], label_ref, class_ref), (x_buf, kernel_buf, u_buf, label_buf, class_buf), sems
    )
    below = jnp.zeros((sub - rows, channels), F32)
    got_x.wait()
    for col in range(cols):
        active_ref[col] = jnp.concatenate([jnp.maximum(column(x_buf, col, channels), 0.0), below], axis=0)
    got_kernel.wait()
    for start, width in tiles(channels):
        at = pl.ds(start, width)
        taps = [kernel_buf[t : t + 1, at].astype(F32) for t in range(9)]
        before = jnp.zeros((sub, width), F32)
        pending = before
        for col in range(cols):
            mid = active_ref[col, :, at]
            up = pltpu.roll(mid, 1, 0)
            down = pltpu.roll(mid, sub - 1, 0)
            sums = [taps[j] * up + taps[3 + j] * mid + taps[6 + j] * down for j in range(3)]
            if col:
                part_ref[col - 1, :, at] = pending + sums[2]
            pending = before + sums[1]
            before = sums[0]
        part_ref[cols - 1, :, at] = pending
    got_u.wait()
    got_label.wait()
    got_class.wait()
    weight = pixel_weights(class_buf, label_buf)
    for col in range(cols):
        grad_ref[col] = jnp.concatenate([column(u_buf, col, channels) * weight[:, col : col + 1], below], axis=0)


def forward_kernel(pieces, rows, where_ref, part_ref, own_ref, one_ref, two_ref, kernel_ref, point_ref, grad_ref, depth_ref, proj_ref, active_ref, stats_ref, part_buf, active_buf, halo_buf, point_buf, kernel_buf, sems):
    cols, sub, channels = part_buf.shape
    got_kernel, got_point = fetches((kernel_ref, point_ref), (kernel_buf, point_buf), sems)
    put_active = pltpu.make_async_copy(active_buf, active_ref, sems.at[2])
    even = where_ref[0] % 2 == 0
    near_line = jnp.where(even, rows, sub - 1)
    far_line = jnp.where(even, sub - 1, rows)
    far_line = jnp.where((where_ref[0] == 0) | (where_ref[0] == pieces - 1), sub, far_line)
    for col in range(cols):
        start = col * channels
        base = start // LANES * LANES
        off = start - base
        end = min(two_ref.shape[1], base + round_up(off + channels, LANES))
        near = one_ref[0, :, base:end].astype(F32)
        one = jnp.where(even, near[:1], near[rows - 1 :])
        two = two_ref[:, base:end].astype(F32)
        line = lax.broadcasted_iota(jnp.int32, (sub, end - base), 0)
        lines = jnp.maximum(jnp.where(line == near_line, one, jnp.where(line == far_line, two, 0.0)), 0.0)
        halo_buf[col] = lines[:, off : off + channels]
    got_kernel.wait()
    line = lax.broadcasted_iota(jnp.int32, (sub, channels), 0)
    wide = [
        jnp.where(line == sub - 1, kernel_buf[j : j + 1, :].astype(F32), kernel_buf[6 + j : 7 + j, :].astype(F32))
        for j in range(3)
    ]
    for start, width in tiles(channels):
        at = pl.ds(start, width)
        row = lax.broadcasted_iota(jnp.int32, (sub, width), 0)
        taps = [w[:, start : start + width] for w in wide]

        def finish(col, value):
            shifted = jnp.where(row == 0, pltpu.roll(value, 1, 0), jnp.where(row == rows - 1, pltpu.roll(value, sub - 1, 0), 0.0))
            total = part_ref[col, :, at] + shifted
            part_buf[col, :, at] = jnp.where(row < rows, total, 0.0)

        before = jnp.zeros((sub, width), F32)
        pending = before
        for col in range(cols):
            halo = halo_buf[col, :, at]
            active_buf[col, :, at] = own_ref[col, :, at] + halo
            if col:
                finish(col - 1, pending + taps[2] * halo)
            pending = before + taps[1] * halo
            before = taps[0] * halo
        finish(cols - 1, pending)
    put_active.start()
    depth = part_buf[...].reshape(cols * sub, channels).astype(BF16)
    depth_ref[:, :channels] = depth
    depth_ref[:, channels:] = jnp.zeros((cols * sub, depth_ref.shape[1] - channels), BF16)
    got_point.wait()
    proj_ref[...] = jnp.dot(depth, point_buf[...], preferred_element_type=F32)
    count = rows * cols
    for start, width in tiles(channels):
        at = pl.ds(start, width)
        proj = proj_ref[:, at]
        grads = grad_ref[:, :, at].reshape(cols * sub, width)
        mine = lax.broadcasted_iota(jnp.int32, (cols * sub, width), 0) % sub < rows
        center = jnp.sum(proj, axis=0, keepdims=True) / count
        deviation = jnp.where(mine, proj - center, 0.0)
        stats_ref[0:1, at] = center
        stats_ref[1:2, at] = jnp.sum(deviation * deviation, axis=0, keepdims=True)
        stats_ref[2:3, at] = jnp.sum(grads, axis=0, keepdims=True)
        stats_ref[3:4, at] = jnp.sum(grads * deviation, axis=0, keepdims=True)
        stats_ref[4:SUB, at] = jnp.zeros((SUB - 4, width), F32)
    put_active.wait()


def paired_sum(values):
    while len(values) > 1:
        values = [sum(values[i : i + 2]) for i in range(0, len(values), 2)]
    return values[0]


def cotangent_kernel(pieces, rows, proj_ref, grad_ref, gain_ref, _, *refs):
    stats_refs, (full_ref, norm_ref) = refs[:-2], refs[-2:]
    cols, sub, channels = grad_ref.shape
    local = rows * cols
    count = local * pieces
    stats = [ref[p : p + 4, :] for ref in stats_refs for p in range(0, ref.shape[0], SUB)]
    center = paired_sum([s[0:1] for s in stats]) / pieces
    square = paired_sum([s[1:2] + local * (s[0:1] - center) ** 2 for s in stats])
    shift_part = paired_sum([s[2:3] for s in stats])
    cross = paired_sum([s[3:4] + (s[0:1] - center) * s[2:3] for s in stats])
    inverse = lax.rsqrt(square / count + EPS)
    gain_part = cross * inverse
    gain = gain_ref[...].reshape(1, channels)
    norm_ref[0:1, :] = center
    norm_ref[1:2, :] = inverse
    norm_ref[2:3, :] = gain_part
    norm_ref[3:4, :] = shift_part
    norm_ref[4:SUB, :] = jnp.zeros((SUB - 4, channels), F32)
    for start, width in tiles(channels):
        at = slice(start, start + width)
        mine = lax.broadcasted_iota(jnp.int32, (cols * sub, width), 0) % sub < rows
        normed = (proj_ref[:, start : start + width] - center[:, at]) * inverse[:, at]
        grads = grad_ref[:, :, start : start + width].reshape(cols * sub, width)
        value = (gain * inverse)[:, at] * (grads - (shift_part / count)[:, at] - normed * (gain_part / count)[:, at])
        full_ref[:, start : start + width] = jnp.where(mine, value, 0.0).astype(BF16)
    full_ref[:, channels:] = jnp.zeros((cols * sub, full_ref.shape[1] - channels), BF16)


def product_kernel(full_ref, depth_ref, out_ref):
    channels = out_ref.shape[1]
    out_ref[...] = lax.dot_general(
        full_ref[:, :channels], depth_ref[:, :channels], (((0,), (0,)), ((), ())), preferred_element_type=F32
    )


def shares_kernel(pieces, share, where_ref, full_ref, depth_ref, own_ref, *refs):
    outs, total_ref = refs[:-1], refs[-1]
    product_kernel(full_ref, depth_ref, total_ref)
    for owner in range(pieces):

        @pl.when(where_ref[0] == owner)
        def _():
            def part(place):
                at = slice(place * share, (place + 1) * share)
                return total_ref[at, :] + own_ref[at, :]

            if pieces == 4:
                keep_ref, send_ref = outs
                keep_ref[...] = part(owner)
                send_ref[...] = part(owner ^ 2).astype(BF16)
            else:
                for j in range(pieces // 2):
                    outs[0][j] = part(2 * j + owner % 2)


def backward_kernel(rows, where_ref, full_ref, point_ref, active_ref, depth_grad_ref, tap_ref, one_ref, two_ref, point_buf, active_buf, grad_buf, sems):
    cols, sub, channels = active_buf.shape
    got_point, got_active = fetches((point_ref, active_ref), (point_buf, active_buf), sems)
    put = pltpu.make_async_copy(grad_buf, depth_grad_ref, sems.at[2])
    got_point.wait()
    grad = lax.dot_general(full_ref[:, :channels], point_buf[...], (((1,), (1,)), ((), ())), preferred_element_type=F32)
    grad_buf[...] = grad.astype(BF16).astype(F32).reshape(cols, sub, channels)
    put.start()
    even = where_ref[0] % 2 == 0
    first = grad_buf[:, 0, :].astype(BF16)
    last = grad_buf[:, rows - 1, :].astype(BF16)
    one_ref[...] = jnp.where(even, last, first)
    two_ref[...] = jnp.where(even, first, last)
    got_active.wait()
    for start, width in tiles(channels):
        at = pl.ds(start, width)
        totals = [jnp.zeros((sub, width), F32) for _ in range(9)]
        zero = jnp.zeros((sub, width), F32)
        ahead = grad_buf[0, :, at]
        here = zero
        for col in range(cols):
            behind, here = here, ahead
            ahead = grad_buf[col + 1, :, at] if col + 1 < cols else zero
            mid = active_buf[col, :, at]
            shifted = (pltpu.roll(mid, 1, 0), mid, pltpu.roll(mid, sub - 1, 0))
            for i in range(3):
                for j, other in enumerate((ahead, here, behind)):
                    totals[3 * i + j] = totals[3 * i + j] + shifted[i] * other
        for t in range(9):
            tap_ref[t : t + 1, at] = jnp.sum(totals[t], axis=0, keepdims=True)
        tap_ref[9:, at] = jnp.zeros((tap_ref.shape[0] - 9, width), F32)
    put.wait()


def fold(small, pieces, owner):
    share = small.shape[1] // pieces
    lines = -(-small.shape[0] // pieces)
    mine = small[:, owner * share : (owner + 1) * share]
    spare = lines * pieces - small.shape[0]
    if spare:
        mine = jnp.concatenate([mine, jnp.zeros((spare, share), F32)], axis=0)
    return jnp.concatenate([mine[q * lines : (q + 1) * lines] for q in range(pieces)], axis=1)


def unfold(lines, pieces, count):
    share = lines.shape[1] // pieces
    return jnp.concatenate([lines[:, q * share : (q + 1) * share] for q in range(pieces)], axis=0)[:count]


def store_halves(ref, start, lines):
    count = lines.shape[0]
    high = lines.astype(BF16).astype(F32)
    ref[start : start + count, :] = high
    ref[start + count : start + 2 * count, :] = lines - high


def small_kernel(pieces, where_ref, taps_ref, other_ref, norm_ref, stay_ref, leave_ref):
    taps = taps_ref[:9, :] + other_ref[:9, :]
    group = norm_ref[2:4, :]
    stay = jnp.concatenate([taps, group], axis=0)
    leave = jnp.concatenate([taps, jnp.zeros_like(group)], axis=0)
    for owner in range(pieces):

        @pl.when(where_ref[0] == owner)
        def _():
            stay_ref[...] = fold(stay, pieces, owner)
            leave_ref[...] = fold(leave, pieces, owner ^ 2)


def fold_kernel(pieces, where_ref, taps_ref, norm_ref, stay_ref, leave_ref):
    step = taps_ref.shape[0] // pieces
    taps = sum(taps_ref[p * step : p * step + 9, :] for p in range(pieces))
    small = jnp.concatenate([taps, norm_ref[2:4, :]], axis=0)
    for owner in range(pieces):

        @pl.when(where_ref[0] == owner)
        def _():
            stay_ref[...] = fold(small, pieces, owner)

    leave_ref[...] = jnp.zeros(leave_ref.shape, F32)


def pack_kernel(keep_ref, came_ref, fold_ref, other_ref, out_ref, flat_ref):
    copies, piece, channels = out_ref.shape
    share, lines = keep_ref.shape[0], fold_ref.shape[0]
    flat_ref[:share, :] = keep_ref[...] + came_ref[...].astype(F32)
    store_halves(flat_ref, share, fold_ref[...] + other_ref[...])
    rest = flat_ref.shape[0] - share - 2 * lines
    if rest:
        flat_ref[share + 2 * lines :, :] = jnp.zeros((rest, channels), F32)
    for k in range(copies):
        out_ref[k] = flat_ref[k * piece : (k + 1) * piece, :].astype(BF16)


def total_kernel(in_ref, out_ref):
    copies = in_ref.shape[0]
    total = in_ref[0].astype(F32)
    for k in range(1, copies):
        total = total + in_ref[k].astype(F32)
    total = total.astype(BF16)
    for k in range(copies):
        out_ref[k] = total


def unpack_kernel(pieces, batch, *refs):
    ins, (point_ref, tap_ref, gain_ref, shift_ref, flat_ref) = refs[:-5], refs[-5:]
    share = point_ref.shape[0]
    start = 0
    for in_ref in ins:
        copies, piece, _ = in_ref.shape
        for k in range(copies):
            flat_ref[start : start + piece, :] = in_ref[k].astype(F32) / batch
            start += piece
    point_ref[...] = flat_ref[:share, :]
    lines = -(-11 // pieces)
    total = flat_ref[share : share + lines, :] + flat_ref[share + lines : share + 2 * lines, :]
    small = unfold(total, pieces, 11)
    tap_ref[...] = small[:9]
    gain_ref[...] = small[9:10].reshape(share)
    shift_ref[...] = small[10:11].reshape(share)


def block_kernel(rows, x_ref, proj_ref, norm_ref, gain_ref, shift_ref, block_ref, x_buf, proj_buf, flat_ref, sems):
    channels = proj_buf.shape[1]
    cols = flat_ref.shape[1] // channels
    sub = proj_buf.shape[0] // cols
    got_x, got_proj = fetches((x_ref.at[0], proj_ref), (x_buf, proj_buf), sems)
    center, inverse = norm_ref[0:1, :], norm_ref[1:2, :]
    gain, shift = gain_ref[...].reshape(1, channels), shift_ref[...].reshape(1, channels)
    got_x.wait()
    got_proj.wait()
    for col in range(cols):
        normed = (proj_buf[col * sub : col * sub + rows, :] - center) * inverse
        result = column(x_buf, col, channels) + gain * normed + shift
        flat_ref[:, col * channels : (col + 1) * channels] = result
    block_ref[...] = flat_ref[...].astype(BF16)


def input_kernel(pieces, rows, where_ref, class_ref, x_ref, u_ref, label_ref, depth_grad_ref, one_ref, two_ref, kernel_ref, input_ref, x_buf, u_buf, halo_buf, flat_ref, class_buf, label_buf, kernel_buf, sems):
    cols, sub, channels = halo_buf.shape
    got_grad, got_kernel, got_x, got_u, got_label, got_class = fetches(
        (depth_grad_ref, kernel_ref, x_ref.at[0], u_ref.at[0], label_ref, class_ref),
        (halo_buf, kernel_buf, x_buf, u_buf, label_buf, class_buf),
        sems,
    )
    even = where_ref[0] % 2 == 0
    has_top = jnp.where(where_ref[0] > 0, 1.0, 0.0)
    has_bottom = jnp.where(where_ref[0] < pieces - 1, 1.0, 0.0)
    one = one_ref[...].astype(F32)
    two = two_ref[...].astype(F32)
    top = jnp.where(even, two, one) * has_top
    bottom = jnp.where(even, one, two) * has_bottom
    line = lax.broadcasted_iota(jnp.int32, (sub, channels), 0)
    got_grad.wait()
    got_kernel.wait()
    for col in range(cols):
        halo_buf[col] = jnp.where(
            line == rows, bottom[col : col + 1], jnp.where(line == sub - 1, top[col : col + 1], halo_buf[col])
        )
    for start, width in tiles(channels):
        at = pl.ds(start, width)
        taps = [kernel_buf[t : t + 1, at].astype(F32) for t in range(9)]
        before = jnp.zeros((sub, width), F32)
        pending = before
        for col in range(cols):
            mid = halo_buf[col, :, at]
            up = pltpu.roll(mid, 1, 0)
            down = pltpu.roll(mid, sub - 1, 0)
            sums = [taps[j] * down + taps[3 + j] * mid + taps[6 + j] * up for j in range(3)]
            if col:
                halo_buf[col - 1, :, at] = pending + sums[0]
            pending = before + sums[1]
            before = sums[2]
        halo_buf[cols - 1, :, at] = pending
    got_x.wait()
    got_u.wait()
    got_label.wait()
    got_class.wait()
    weight = pixel_weights(class_buf, label_buf)
    for col in range(cols):
        grads = column(u_buf, col, channels) * weight[:, col : col + 1]
        image = column(x_buf, col, channels)
        flat_ref[:, col * channels : (col + 1) * channels] = grads + jnp.where(image > 0, halo_buf[col, :rows, :], 0.0)
    input_ref[...] = flat_ref[...].astype(BF16)


def call(body, ins, outs, scratch=(), megabytes=16):
    space = {
        "o": pl.BlockSpec(memory_space=pl.ANY),
        "v": pl.BlockSpec(memory_space=pltpu.VMEM),
        "s": pl.BlockSpec(memory_space=pltpu.SMEM),
        "a": pl.BlockSpec(memory_space=pl.ANY),
    }
    return pl.pallas_call(
        body,
        out_shape=[pltpu.HBM(shape, dtype) if s == "a" else jax.ShapeDtypeStruct(shape, dtype) for s, shape, dtype in outs],
        in_specs=[space[s] for s, _ in ins],
        out_specs=[space[s] for s, _, _ in outs],
        scratch_shapes=list(scratch),
        compiler_params=pltpu.CompilerParams(vmem_limit_bytes=megabytes * 1024 * 1024),
    )(*[pltpu.with_memory_space_constraint(a, pltpu.HBM) if s == "a" else a for s, a in ins])


def local(inputs, upstream, labels, class_weights, depth_kernel, point_weight, gain, shift):
    samples, rows, flat = inputs.shape
    assert samples == 1
    channels = point_weight.shape[0]
    cols = flat // channels
    pieces = lax.axis_size("slab")
    copies = lax.axis_size("dp")
    assert pieces % 2 == 0
    share = channels // pieces
    sub = round_up(rows + 2, SUB)
    padded = round_up(channels, LANES)
    me = lax.axis_index("slab")
    where = me.astype(jnp.int32).reshape(1)
    even = me % 2 == 0
    image = inputs.reshape(rows, flat)
    near = [(i, i ^ 1) for i in range(pieces)]
    far = [(i, (i - 1) % pieces if i % 2 == 0 else (i + 1) % pieces) for i in range(pieces)]
    lane3 = (cols, sub, channels)
    pixels = cols * sub
    buf3 = pltpu.VMEM(lane3, F32)
    flat_buf = pltpu.VMEM((rows, flat), BF16)
    flat_f32 = pltpu.VMEM((rows, flat), F32)
    point_buf = pltpu.VMEM((channels, channels), BF16)
    kernel_buf = pltpu.VMEM(depth_kernel.shape, BF16)
    label_buf = pltpu.VMEM((rows, 1, cols), labels.dtype)
    label_lines = jnp.transpose(labels, (1, 0, 2))
    class_buf = pltpu.SMEM(class_weights.shape, F32)

    one = lax.ppermute(inputs, "slab", near)
    two = lax.ppermute(lax.dynamic_slice_in_dim(image, jnp.where(even, 0, rows - 1), 1, 0), "slab", far)
    own, part, grad_out = call(
        prepare_kernel,
        [("a", class_weights), ("a", inputs), ("a", upstream), ("a", label_lines), ("a", depth_kernel)],
        [("v", lane3, F32), ("v", lane3, F32), ("v", lane3, F32)],
        [class_buf, flat_buf, flat_buf, label_buf, kernel_buf, DMA((5,))],
        megabytes=16,
    )
    depth, projected, active, stats = call(
        functools.partial(forward_kernel, pieces, rows),
        [("s", where), ("v", part), ("v", own), ("v", one), ("v", two), ("a", depth_kernel), ("a", point_weight), ("v", grad_out)],
        [("v", (pixels, padded), BF16), ("v", (pixels, channels), F32), ("a", lane3, F32), ("v", (SUB, channels), F32)],
        [buf3, buf3, buf3, point_buf, kernel_buf, DMA((3,))],
    )
    other_depth = lax.ppermute(depth, "slab", near)
    across = [(i, i ^ 2) for i in range(pieces)]
    if pieces == 4:
        apart = [(i, i ^ 3) for i in range(pieces)]
        all_stats = [stats, *(lax.ppermute(stats, "slab", pairs) for pairs in (near, across, apart))]
    else:
        all_stats = [lax.all_gather(stats, "slab", axis=0, tiled=True)]
    full, norm = call(
        functools.partial(cotangent_kernel, pieces, rows),
        [("v", projected), ("v", grad_out), ("v", gain), ("o", other_depth), *(("v", part) for part in all_stats)],
        [("v", (pixels, padded), BF16), ("v", (SUB, channels), F32)],
    )
    theirs = lax.ppermute(full, "slab", near)
    (own_product,) = call(product_kernel, [("v", full), ("v", depth)], [("v", (channels, channels), F32)])
    lines = -(-11 // pieces)
    batch = samples * copies
    if pieces == 4:
        share_outs = [("v", (share, channels), F32), ("v", (share, channels), BF16)]
    else:
        share_outs = [("v", (pieces // 2, share, channels), F32)]
    products = call(
        functools.partial(shares_kernel, pieces, share),
        [("s", where), ("v", theirs), ("v", other_depth), ("v", own_product)],
        share_outs,
        [pltpu.VMEM((channels, channels), F32)],
    )
    if pieces == 4:
        keep, leaving = products
    else:
        blocks = products[0]
        while blocks.shape[0] > 2:
            half = blocks.shape[0] // 2
            high = ((me // 2) & half) != 0
            mine = lax.dynamic_slice_in_dim(blocks, jnp.where(high, half, 0), half, 0)
            leaving = lax.dynamic_slice_in_dim(blocks, jnp.where(high, 0, half), half, 0).astype(BF16)
            came = lax.ppermute(leaving, "slab", [(i, i ^ (2 * half)) for i in range(pieces)])
            blocks = mine + came.astype(F32)
        bit = (me // 2) % 2
        keep = blocks[0] if pieces == 2 else lax.dynamic_index_in_dim(blocks, bit, 0, False)
        leaving = None if pieces == 2 else lax.dynamic_index_in_dim(blocks, 1 - bit, 0, False).astype(BF16)
    if pieces > 2:
        leaving, full = lax.optimization_barrier((leaving, full))
        came = lax.ppermute(leaving, "slab", across)
    else:
        came = jnp.zeros((share, channels), BF16)
    depth_grad, taps, edge_one, edge_two = call(
        functools.partial(backward_kernel, rows),
        [("s", where), ("v", full), ("o", point_weight), ("o", active)],
        [("a", lane3, F32), ("v", (2 * SUB, channels), F32), ("v", (cols, channels), BF16), ("v", (cols, channels), BF16)],
        [point_buf, buf3, buf3, DMA((3,))],
    )
    fold_outs = [("v", (lines, channels), F32)] * 2
    if pieces == 4:
        stay, leave = call(
            functools.partial(small_kernel, pieces),
            [("s", where), ("v", taps), ("v", lax.ppermute(taps, "slab", near)), ("v", norm)],
            fold_outs,
        )
        leave, norm = lax.optimization_barrier((leave, norm))
        leave = lax.ppermute(leave, "slab", across)
    else:
        all_taps = lax.all_gather(taps, "slab", axis=0, tiled=True)
        stay, leave = call(functools.partial(fold_kernel, pieces), [("s", where), ("v", all_taps), ("v", norm)], fold_outs)
    (block_out,) = call(
        functools.partial(block_kernel, rows),
        [("a", inputs), ("o", projected), ("v", norm), ("v", gain), ("v", shift)],
        [("v", (rows, flat), BF16)],
        [flat_buf, pltpu.VMEM((pixels, channels), F32), flat_f32, DMA((2,))],
    )
    piece = -(-(share + 2 * lines) // copies)
    total = piece * copies
    (packed,) = call(
        pack_kernel,
        [("v", keep), ("v", came), ("v", stay), ("v", leave)],
        [("v", (copies, piece, channels), BF16)],
        [pltpu.VMEM((total, channels), F32)],
    )
    landed = lax.all_to_all(packed, "dp", 0, 0)
    (summed,) = call(total_kernel, [("v", landed)], [("v", packed.shape, BF16)])
    gathered = lax.all_to_all(summed, "dp", 0, 0)
    halo_one = lax.ppermute(edge_one, "slab", near)
    halo_two = lax.ppermute(edge_two, "slab", far)
    (grad_input,) = call(
        functools.partial(input_kernel, pieces, rows),
        [("s", where), ("a", class_weights), ("a", inputs), ("a", upstream), ("a", label_lines), ("a", depth_grad), ("v", halo_one), ("v", halo_two), ("a", depth_kernel)],
        [("v", (rows, flat), BF16)],
        [flat_buf, flat_buf, buf3, flat_f32, class_buf, label_buf, kernel_buf, DMA((6,))],
    )
    point_out, tap_out, gain_out, shift_out = call(
        functools.partial(unpack_kernel, pieces, batch),
        [("v", gathered)],
        [("v", (share, channels), F32), ("v", (9, share), F32), ("v", (share,), F32), ("v", (share,), F32)],
        [pltpu.VMEM((total, channels), F32)],
    )
    return (
        block_out.reshape(inputs.shape),
        grad_input.reshape(inputs.shape),
        point_out.T,
        tap_out,
        gain_out,
        shift_out,
    )


def solution(mesh):
    return jax.shard_map(
        local,
        mesh=mesh,
        in_specs=(
            P("dp", "slab", None),
            P("dp", "slab", None),
            P("dp", "slab", None),
            P(),
            P(),
            P(),
            P(),
            P(),
        ),
        out_specs=(
            P("dp", "slab", None),
            P("dp", "slab", None),
            P(None, "slab"),
            P(None, "slab"),
            P("slab"),
            P("slab"),
        ),
        check_vma=False,
    )
```

```python
import functools

import jax
import jax.numpy as jnp
from jax import lax
from jax.experimental import pallas as pl
from jax.experimental.pallas import tpu as pltpu
from jax.sharding import PartitionSpec as P

F32 = jnp.float32
BF16 = jnp.bfloat16
LANES = 128
SUB = 8
EPS = 1e-05
DMA = pltpu.SemaphoreType.DMA


def round_up(value, unit):
    return -(-value // unit) * unit


def tiles(width):
    return [(start, min(LANES, width - start)) for start in range(0, width, LANES)]


def column(ref, col, channels, scale=None):
    start = col * channels
    base = start // LANES * LANES
    off = start - base
    end = min(ref.shape[1], base + round_up(off + channels, LANES))
    values = ref[:, base:end].astype(F32)
    if scale is not None:
        values = values * jnp.concatenate([scale] * ((end - base) // LANES), axis=1)
    return values[:, off : off + channels]


def pixel_weights(class_ref, label_ref):
    labels = jnp.concatenate([label_ref[r] for r in range(label_ref.shape[0])], axis=0)
    weight = jnp.zeros(labels.shape, F32)
    for t in range(class_ref.shape[0]):
        weight = jnp.where(labels == t, class_ref[t], weight)
    return weight


def spread_weights(ref, weight):
    for col in range(ref.shape[0]):
        ref[col] = jnp.broadcast_to(weight[:, col : col + 1], ref.shape[1:])


def fetches(sources, buffers, sems):
    copies = [pltpu.make_async_copy(s, b, sems.at[i]) for i, (s, b) in enumerate(zip(sources, buffers))]
    for copy in copies:
        copy.start()
    return copies


def prepare_kernel(class_ref, x_ref, u_ref, label_ref, kernel_ref, active_ref, part_ref, grad_ref, class_buf, x_buf, u_buf, label_buf, kernel_buf, weight_buf, sems):
    rows, _, cols = label_buf.shape
    sub, channels = grad_ref.shape[1:]
    got_x, got_kernel, got_u, got_label, got_class = fetches(
        (x_ref.at[0], kernel_ref, u_ref.at[0], label_ref, class_ref), (x_buf, kernel_buf, u_buf, label_buf, class_buf), sems
    )
    below = jnp.zeros((sub - rows, channels), F32)
    got_x.wait()
    for col in range(cols):
        active_ref[col] = jnp.concatenate([jnp.maximum(column(x_buf, col, channels), 0.0), below], axis=0)
    got_kernel.wait()
    for start, width in tiles(channels):
        at = pl.ds(start, width)
        taps = [kernel_buf[t : t + 1, at].astype(F32) for t in range(9)]
        before = jnp.zeros((sub, width), F32)
        pending = before
        for col in range(cols):
            mid = active_ref[col, :, at]
            up = pltpu.roll(mid, 1, 0)
            down = pltpu.roll(mid, sub - 1, 0)
            sums = [taps[j] * up + taps[3 + j] * mid + taps[6 + j] * down for j in range(3)]
            if col:
                part_ref[col - 1, :, at] = pending + sums[2]
            pending = before + sums[1]
            before = sums[0]
        part_ref[cols - 1, :, at] = pending
    got_u.wait()
    got_label.wait()
    got_class.wait()
    spread_weights(weight_buf, pixel_weights(class_buf, label_buf))
    for col in range(cols):
        grad_ref[col] = jnp.concatenate([column(u_buf, col, channels, weight_buf[col]), below], axis=0)


def forward_kernel(pieces, rows, where_ref, part_ref, own_ref, one_ref, two_ref, kernel_ref, point_ref, grad_ref, depth_ref, proj_ref, active_ref, stats_ref, part_buf, halo_buf, line_buf):
    cols, sub, channels = part_buf.shape
    even = where_ref[0] % 2 == 0
    near_line = jnp.where(even, rows, sub - 1)
    far_line = jnp.where(even, sub - 1, rows)
    far_line = jnp.where((where_ref[0] == 0) | (where_ref[0] == pieces - 1), sub, far_line)
    line_buf[...] = two_ref[...].astype(F32)
    for col in range(cols):
        start = col * channels
        base = start // LANES * LANES
        off = start - base
        end = min(one_ref.shape[2], base + round_up(off + channels, LANES))
        near = one_ref[0, :, base:end].astype(F32)
        one = jnp.where(even, near[:1], near[rows - 1 :])
        parts = [line_buf[t : t + 1, :] for t in range(base // LANES, -(-end // LANES))]
        two = jnp.concatenate(parts, axis=1)[:, : end - base]
        line = lax.broadcasted_iota(jnp.int32, (sub, end - base), 0)
        lines = jnp.maximum(jnp.where(line == near_line, one, jnp.where(line == far_line, two, 0.0)), 0.0)
        halo_buf[col] = lines[:, off : off + channels]
    line = lax.broadcasted_iota(jnp.int32, (sub, channels), 0)
    wide = [
        jnp.where(line == sub - 1, kernel_ref[j : j + 1, :].astype(F32), kernel_ref[6 + j : 7 + j, :].astype(F32))
        for j in range(3)
    ]
    for start, width in tiles(channels):
        at = pl.ds(start, width)
        row = lax.broadcasted_iota(jnp.int32, (sub, width), 0)
        taps = [w[:, start : start + width] for w in wide]

        def finish(col, value):
            shifted = jnp.where(row == 0, pltpu.roll(value, 1, 0), jnp.where(row == rows - 1, pltpu.roll(value, sub - 1, 0), 0.0))
            total = part_ref[col, :, at] + shifted
            part_buf[col, :, at] = jnp.where(row < rows, total, 0.0)

        before = jnp.zeros((sub, width), F32)
        pending = before
        for col in range(cols):
            halo = halo_buf[col, :, at]
            active_ref[col, :, at] = own_ref[col, :, at] + halo
            if col:
                finish(col - 1, pending + taps[2] * halo)
            pending = before + taps[1] * halo
            before = taps[0] * halo
        finish(cols - 1, pending)
    depth = part_buf[...].reshape(cols * sub, channels).astype(BF16)
    depth_ref[:, :channels] = depth
    depth_ref[:, channels:] = jnp.zeros((cols * sub, depth_ref.shape[1] - channels), BF16)
    proj_ref[...] = jnp.dot(depth, point_ref[...], preferred_element_type=F32)
    count = rows * cols
    for start, width in tiles(channels):
        at = pl.ds(start, width)
        proj = proj_ref[:, at]
        grads = grad_ref[:, :, at].reshape(cols * sub, width)
        mine = lax.broadcasted_iota(jnp.int32, (cols * sub, width), 0) % sub < rows
        center = jnp.sum(proj, axis=0, keepdims=True) / count
        deviation = jnp.where(mine, proj - center, 0.0)
        stats_ref[0:1, at] = center
        stats_ref[1:2, at] = jnp.sum(deviation * deviation, axis=0, keepdims=True)
        stats_ref[2:3, at] = jnp.sum(grads, axis=0, keepdims=True)
        stats_ref[3:4, at] = jnp.sum(grads * deviation, axis=0, keepdims=True)
        stats_ref[4:SUB, at] = jnp.zeros((SUB - 4, width), F32)


def paired_sum(values):
    while len(values) > 1:
        values = [sum(values[i : i + 2]) for i in range(0, len(values), 2)]
    return values[0]


def cotangent_kernel(pieces, rows, proj_ref, grad_ref, gain_ref, _, *refs):
    stats_refs, (full_ref, norm_ref) = refs[:-2], refs[-2:]
    cols, sub, channels = grad_ref.shape
    local = rows * cols
    count = local * pieces
    stats = [ref[p : p + 4, :] for ref in stats_refs for p in range(0, ref.shape[0], SUB)]
    center = paired_sum([s[0:1] for s in stats]) / pieces
    square = paired_sum([s[1:2] + local * (s[0:1] - center) ** 2 for s in stats])
    shift_part = paired_sum([s[2:3] for s in stats])
    cross = paired_sum([s[3:4] + (s[0:1] - center) * s[2:3] for s in stats])
    inverse = lax.rsqrt(square / count + EPS)
    gain_part = cross * inverse
    gain = gain_ref[...].reshape(1, channels)
    norm_ref[0:1, :] = center
    norm_ref[1:2, :] = inverse
    norm_ref[2:3, :] = gain_part
    norm_ref[3:4, :] = shift_part
    norm_ref[4:SUB, :] = jnp.zeros((SUB - 4, channels), F32)
    for start, width in tiles(channels):
        at = slice(start, start + width)
        mine = lax.broadcasted_iota(jnp.int32, (cols * sub, width), 0) % sub < rows
        normed = (proj_ref[:, start : start + width] - center[:, at]) * inverse[:, at]
        grads = grad_ref[:, :, start : start + width].reshape(cols * sub, width)
        value = (gain * inverse)[:, at] * (grads - (shift_part / count)[:, at] - normed * (gain_part / count)[:, at])
        full_ref[:, start : start + width] = jnp.where(mine, value, 0.0).astype(BF16)
    full_ref[:, channels:] = jnp.zeros((cols * sub, full_ref.shape[1] - channels), BF16)


def product_kernel(full_ref, depth_ref, out_ref):
    channels = out_ref.shape[1]
    out_ref[...] = lax.dot_general(
        full_ref[:, :channels], depth_ref[:, :channels], (((0,), (0,)), ((), ())), preferred_element_type=F32
    )


def shares_kernel(pieces, share, where_ref, full_ref, depth_ref, own_ref, *refs):
    outs, total_ref = refs[:-1], refs[-1]
    product_kernel(full_ref, depth_ref, total_ref)
    for owner in range(pieces):

        @pl.when(where_ref[0] == owner)
        def _():
            def part(place):
                at = slice(place * share, (place + 1) * share)
                return total_ref[at, :] + own_ref[at, :]

            if pieces == 4:
                keep_ref, send_ref = outs
                keep_ref[...] = part(owner)
                send_ref[...] = part(owner ^ 2).astype(BF16)
            else:
                for j in range(pieces // 2):
                    outs[0][j] = part(2 * j + owner % 2)


def backward_kernel(rows, where_ref, full_ref, point_ref, active_ref, depth_grad_ref, tap_ref, one_ref, two_ref, point_buf, active_buf, grad_buf, sems):
    cols, sub, channels = active_buf.shape
    got_point, got_active = fetches((point_ref, active_ref), (point_buf, active_buf), sems)
    put = pltpu.make_async_copy(grad_buf, depth_grad_ref, sems.at[2])
    got_point.wait()
    grad = lax.dot_general(full_ref[:, :channels], point_buf[...], (((1,), (1,)), ((), ())), preferred_element_type=F32)
    grad_buf[...] = grad.astype(BF16).astype(F32).reshape(cols, sub, channels)
    put.start()
    even = where_ref[0] % 2 == 0
    first = grad_buf[:, 0, :].astype(BF16)
    last = grad_buf[:, rows - 1, :].astype(BF16)
    one_ref[...] = jnp.where(even, last, first)
    two_ref[...] = jnp.where(even, first, last)
    got_active.wait()
    for start, width in tiles(channels):
        at = pl.ds(start, width)
        totals = [jnp.zeros((sub, width), F32) for _ in range(9)]
        zero = jnp.zeros((sub, width), F32)
        ahead = grad_buf[0, :, at]
        here = zero
        for col in range(cols):
            behind, here = here, ahead
            ahead = grad_buf[col + 1, :, at] if col + 1 < cols else zero
            mid = active_buf[col, :, at]
            shifted = (pltpu.roll(mid, 1, 0), mid, pltpu.roll(mid, sub - 1, 0))
            for i in range(3):
                for j, other in enumerate((ahead, here, behind)):
                    totals[3 * i + j] = totals[3 * i + j] + shifted[i] * other
        for t in range(9):
            tap_ref[t : t + 1, at] = jnp.sum(totals[t], axis=0, keepdims=True)
        tap_ref[9:, at] = jnp.zeros((tap_ref.shape[0] - 9, width), F32)
    put.wait()


def fold(small, pieces, owner):
    share = small.shape[1] // pieces
    lines = -(-small.shape[0] // pieces)
    mine = small[:, owner * share : (owner + 1) * share]
    spare = lines * pieces - small.shape[0]
    if spare:
        mine = jnp.concatenate([mine, jnp.zeros((spare, share), F32)], axis=0)
    return jnp.concatenate([mine[q * lines : (q + 1) * lines] for q in range(pieces)], axis=1)


def unfold(lines, pieces, count):
    share = lines.shape[1] // pieces
    return jnp.concatenate([lines[:, q * share : (q + 1) * share] for q in range(pieces)], axis=0)[:count]


def store_halves(ref, start, lines):
    count = lines.shape[0]
    high = lines.astype(BF16).astype(F32)
    ref[start : start + count, :] = high
    ref[start + count : start + 2 * count, :] = lines - high


def small_kernel(pieces, where_ref, taps_ref, other_ref, norm_ref, stay_ref, leave_ref):
    taps = taps_ref[:9, :] + other_ref[:9, :]
    group = norm_ref[2:4, :]
    stay = jnp.concatenate([taps, group], axis=0)
    leave = jnp.concatenate([taps, jnp.zeros_like(group)], axis=0)
    for owner in range(pieces):

        @pl.when(where_ref[0] == owner)
        def _():
            stay_ref[...] = fold(stay, pieces, owner)
            leave_ref[...] = fold(leave, pieces, owner ^ 2)


def fold_kernel(pieces, where_ref, taps_ref, norm_ref, stay_ref, leave_ref):
    step = taps_ref.shape[0] // pieces
    taps = sum(taps_ref[p * step : p * step + 9, :] for p in range(pieces))
    small = jnp.concatenate([taps, norm_ref[2:4, :]], axis=0)
    for owner in range(pieces):

        @pl.when(where_ref[0] == owner)
        def _():
            stay_ref[...] = fold(small, pieces, owner)

    leave_ref[...] = jnp.zeros(leave_ref.shape, F32)


def pack_kernel(keep_ref, came_ref, fold_ref, other_ref, out_ref, flat_ref):
    copies, piece, channels = out_ref.shape
    share, lines = keep_ref.shape[0], fold_ref.shape[0]
    flat_ref[:share, :] = keep_ref[...] + came_ref[...].astype(F32)
    store_halves(flat_ref, share, fold_ref[...] + other_ref[...])
    rest = flat_ref.shape[0] - share - 2 * lines
    if rest:
        flat_ref[share + 2 * lines :, :] = jnp.zeros((rest, channels), F32)
    for k in range(copies):
        out_ref[k] = flat_ref[k * piece : (k + 1) * piece, :].astype(BF16)


def total_kernel(in_ref, out_ref):
    copies = in_ref.shape[0]
    total = in_ref[0].astype(F32)
    for k in range(1, copies):
        total = total + in_ref[k].astype(F32)
    total = total.astype(BF16)
    for k in range(copies):
        out_ref[k] = total


def unpack_kernel(pieces, batch, *refs):
    ins, (point_ref, tap_ref, gain_ref, shift_ref, flat_ref) = refs[:-5], refs[-5:]
    share = point_ref.shape[0]
    start = 0
    for in_ref in ins:
        copies, piece, _ = in_ref.shape
        for k in range(copies):
            flat_ref[start : start + piece, :] = in_ref[k].astype(F32) / batch
            start += piece
    point_ref[...] = flat_ref[:share, :]
    lines = -(-11 // pieces)
    total = flat_ref[share : share + lines, :] + flat_ref[share + lines : share + 2 * lines, :]
    small = unfold(total, pieces, 11)
    tap_ref[...] = small[:9]
    gain_ref[...] = small[9:10].reshape(share)
    shift_ref[...] = small[10:11].reshape(share)


def block_kernel(rows, x_ref, proj_ref, norm_ref, gain_ref, shift_ref, block_ref, x_buf, proj_buf, flat_ref, sems):
    channels = proj_buf.shape[1]
    cols = flat_ref.shape[1] // channels
    sub = proj_buf.shape[0] // cols
    got_x, got_proj = fetches((x_ref.at[0], proj_ref), (x_buf, proj_buf), sems)
    center, inverse = norm_ref[0:1, :], norm_ref[1:2, :]
    gain, shift = gain_ref[...].reshape(1, channels), shift_ref[...].reshape(1, channels)
    got_x.wait()
    got_proj.wait()
    for col in range(cols):
        normed = (proj_buf[col * sub : col * sub + rows, :] - center) * inverse
        result = column(x_buf, col, channels) + gain * normed + shift
        flat_ref[:, col * channels : (col + 1) * channels] = result
    block_ref[...] = flat_ref[...].astype(BF16)


def input_kernel(pieces, rows, where_ref, class_ref, x_ref, u_ref, label_ref, depth_grad_ref, one_ref, two_ref, kernel_ref, input_ref, x_buf, u_buf, halo_buf, flat_ref, class_buf, label_buf, kernel_buf, weight_buf, sems):
    cols, sub, channels = halo_buf.shape
    got_grad, got_kernel, got_x, got_u, got_label, got_class = fetches(
        (depth_grad_ref, kernel_ref, x_ref.at[0], u_ref.at[0], label_ref, class_ref),
        (halo_buf, kernel_buf, x_buf, u_buf, label_buf, class_buf),
        sems,
    )
    even = where_ref[0] % 2 == 0
    has_top = jnp.where(where_ref[0] > 0, 1.0, 0.0)
    has_bottom = jnp.where(where_ref[0] < pieces - 1, 1.0, 0.0)
    one = one_ref[...].astype(F32)
    two = two_ref[...].astype(F32)
    top = jnp.where(even, two, one) * has_top
    bottom = jnp.where(even, one, two) * has_bottom
    line = lax.broadcasted_iota(jnp.int32, (sub, channels), 0)
    got_grad.wait()
    got_kernel.wait()
    for col in range(cols):
        halo_buf[col] = jnp.where(
            line == rows, bottom[col : col + 1], jnp.where(line == sub - 1, top[col : col + 1], halo_buf[col])
        )
    for start, width in tiles(channels):
        at = pl.ds(start, width)
        taps = [kernel_buf[t : t + 1, at].astype(F32) for t in range(9)]
        before = jnp.zeros((sub, width), F32)
        pending = before
        for col in range(cols):
            mid = halo_buf[col, :, at]
            up = pltpu.roll(mid, 1, 0)
            down = pltpu.roll(mid, sub - 1, 0)
            sums = [taps[j] * down + taps[3 + j] * mid + taps[6 + j] * up for j in range(3)]
            if col:
                halo_buf[col - 1, :, at] = pending + sums[0]
            pending = before + sums[1]
            before = sums[2]
        halo_buf[cols - 1, :, at] = pending
    got_x.wait()
    got_u.wait()
    got_label.wait()
    got_class.wait()
    spread_weights(weight_buf, pixel_weights(class_buf, label_buf))
    for col in range(cols):
        grads = column(u_buf, col, channels, weight_buf[col])
        image = column(x_buf, col, channels)
        flat_ref[:, col * channels : (col + 1) * channels] = grads + jnp.where(image > 0, halo_buf[col, :rows, :], 0.0)
    input_ref[...] = flat_ref[...].astype(BF16)


def call(body, ins, outs, scratch=(), megabytes=16):
    space = {
        "o": pl.BlockSpec(memory_space=pl.ANY),
        "v": pl.BlockSpec(memory_space=pltpu.VMEM),
        "s": pl.BlockSpec(memory_space=pltpu.SMEM),
        "a": pl.BlockSpec(memory_space=pl.ANY),
    }
    return pl.pallas_call(
        body,
        out_shape=[pltpu.HBM(shape, dtype) if s == "a" else jax.ShapeDtypeStruct(shape, dtype) for s, shape, dtype in outs],
        in_specs=[space[s] for s, _ in ins],
        out_specs=[space[s] for s, _, _ in outs],
        scratch_shapes=list(scratch),
        compiler_params=pltpu.CompilerParams(vmem_limit_bytes=megabytes * 1024 * 1024),
    )(*[pltpu.with_memory_space_constraint(a, pltpu.HBM) if s == "a" else a for s, a in ins])


def local(inputs, upstream, labels, class_weights, depth_kernel, point_weight, gain, shift):
    samples, rows, flat = inputs.shape
    assert samples == 1
    channels = point_weight.shape[0]
    cols = flat // channels
    pieces = lax.axis_size("slab")
    copies = lax.axis_size("dp")
    assert pieces % 2 == 0
    share = channels // pieces
    sub = round_up(rows + 2, SUB)
    padded = round_up(channels, LANES)
    me = lax.axis_index("slab")
    where = me.astype(jnp.int32).reshape(1)
    even = me % 2 == 0
    image = inputs.reshape(rows, flat)
    near = [(i, i ^ 1) for i in range(pieces)]
    far = [(i, (i - 1) % pieces if i % 2 == 0 else (i + 1) % pieces) for i in range(pieces)]
    lane3 = (cols, sub, channels)
    pixels = cols * sub
    buf3 = pltpu.VMEM(lane3, F32)
    flat_buf = pltpu.VMEM((rows, flat), BF16)
    flat_f32 = pltpu.VMEM((rows, flat), F32)
    point_buf = pltpu.VMEM((channels, channels), BF16)
    kernel_buf = pltpu.VMEM(depth_kernel.shape, BF16)
    label_buf = pltpu.VMEM((rows, 1, cols), labels.dtype)
    label_lines = jnp.transpose(labels, (1, 0, 2))
    weight_buf = pltpu.VMEM((cols, rows, LANES), F32)
    class_buf = pltpu.SMEM(class_weights.shape, F32)

    one = lax.ppermute(inputs, "slab", near)
    edge = jnp.where(even, image[0], image[rows - 1])
    two = lax.ppermute(jnp.pad(edge, (0, -flat % LANES)).reshape(-1, LANES), "slab", far)
    own, part, grad_out = call(
        prepare_kernel,
        [("a", class_weights), ("a", inputs), ("a", upstream), ("a", label_lines), ("a", depth_kernel)],
        [("v", lane3, F32), ("v", lane3, F32), ("v", lane3, F32)],
        [class_buf, flat_buf, flat_buf, label_buf, kernel_buf, weight_buf, DMA((5,))],
        megabytes=16,
    )
    depth, projected, active, stats = call(
        functools.partial(forward_kernel, pieces, rows),
        [("s", where), ("v", part), ("v", own), ("v", one), ("v", two), ("v", depth_kernel), ("v", point_weight), ("v", grad_out)],
        [("v", (pixels, padded), BF16), ("v", (pixels, channels), F32), ("v", lane3, F32), ("v", (SUB, channels), F32)],
        [buf3, buf3, pltpu.VMEM(two.shape, F32)],
    )
    other_depth = lax.ppermute(depth, "slab", near)
    across = [(i, i ^ 2) for i in range(pieces)]
    if pieces == 4:
        apart = [(i, i ^ 3) for i in range(pieces)]
        all_stats = [stats, *(lax.ppermute(stats, "slab", pairs) for pairs in (near, across, apart))]
    else:
        all_stats = [lax.all_gather(stats, "slab", axis=0, tiled=True)]
    full, norm = call(
        functools.partial(cotangent_kernel, pieces, rows),
        [("v", projected), ("v", grad_out), ("v", gain), ("o", other_depth), *(("v", part) for part in all_stats)],
        [("v", (pixels, padded), BF16), ("v", (SUB, channels), F32)],
    )
    theirs = lax.ppermute(full, "slab", near)
    (own_product,) = call(product_kernel, [("v", full), ("v", depth)], [("v", (channels, channels), F32)])
    lines = -(-11 // pieces)
    batch = samples * copies
    if pieces == 4:
        share_outs = [("v", (share, channels), F32), ("v", (share, channels), BF16)]
    else:
        share_outs = [("v", (pieces // 2, share, channels), F32)]
    products = call(
        functools.partial(shares_kernel, pieces, share),
        [("s", where), ("v", theirs), ("v", other_depth), ("v", own_product)],
        share_outs,
        [pltpu.VMEM((channels, channels), F32)],
    )
    if pieces == 4:
        keep, leaving = products
    else:
        blocks = products[0]
        while blocks.shape[0] > 2:
            half = blocks.shape[0] // 2
            high = ((me // 2) & half) != 0
            mine = lax.dynamic_slice_in_dim(blocks, jnp.where(high, half, 0), half, 0)
            leaving = lax.dynamic_slice_in_dim(blocks, jnp.where(high, 0, half), half, 0).astype(BF16)
            came = lax.ppermute(leaving, "slab", [(i, i ^ (2 * half)) for i in range(pieces)])
            blocks = mine + came.astype(F32)
        bit = (me // 2) % 2
        keep = blocks[0] if pieces == 2 else lax.dynamic_index_in_dim(blocks, bit, 0, False)
        leaving = None if pieces == 2 else lax.dynamic_index_in_dim(blocks, 1 - bit, 0, False).astype(BF16)
    if pieces > 2:
        leaving, full = lax.optimization_barrier((leaving, full))
        came = lax.ppermute(leaving, "slab", across)
    else:
        came = jnp.zeros((share, channels), BF16)
    depth_grad, taps, edge_one, edge_two = call(
        functools.partial(backward_kernel, rows),
        [("s", where), ("v", full), ("o", point_weight), ("o", active)],
        [("a", lane3, F32), ("v", (2 * SUB, channels), F32), ("v", (cols, channels), BF16), ("v", (cols, channels), BF16)],
        [point_buf, buf3, buf3, DMA((3,))],
    )
    fold_outs = [("v", (lines, channels), F32)] * 2
    if pieces == 4:
        stay, leave = call(
            functools.partial(small_kernel, pieces),
            [("s", where), ("v", taps), ("v", lax.ppermute(taps, "slab", near)), ("v", norm)],
            fold_outs,
        )
        leave, norm = lax.optimization_barrier((leave, norm))
        leave = lax.ppermute(leave, "slab", across)
    else:
        all_taps = lax.all_gather(taps, "slab", axis=0, tiled=True)
        stay, leave = call(functools.partial(fold_kernel, pieces), [("s", where), ("v", all_taps), ("v", norm)], fold_outs)
    (block_out,) = call(
        functools.partial(block_kernel, rows),
        [("a", inputs), ("o", projected), ("v", norm), ("v", gain), ("v", shift)],
        [("v", (rows, flat), BF16)],
        [flat_buf, pltpu.VMEM((pixels, channels), F32), flat_f32, DMA((2,))],
    )
    piece = -(-(share + 2 * lines) // copies)
    total = piece * copies
    (packed,) = call(
        pack_kernel,
        [("v", keep), ("v", came), ("v", stay), ("v", leave)],
        [("v", (copies, piece, channels), BF16)],
        [pltpu.VMEM((total, channels), F32)],
    )
    landed = lax.all_to_all(packed, "dp", 0, 0)
    (summed,) = call(total_kernel, [("v", landed)], [("v", packed.shape, BF16)])
    gathered = lax.all_to_all(summed, "dp", 0, 0)
    halo_one = lax.ppermute(edge_one, "slab", near)
    halo_two = lax.ppermute(edge_two, "slab", far)
    (grad_input,) = call(
        functools.partial(input_kernel, pieces, rows),
        [("s", where), ("a", class_weights), ("a", inputs), ("a", upstream), ("a", label_lines), ("a", depth_grad), ("v", halo_one), ("v", halo_two), ("a", depth_kernel)],
        [("v", (rows, flat), BF16)],
        [flat_buf, flat_buf, buf3, flat_f32, class_buf, label_buf, kernel_buf, weight_buf, DMA((6,))],
    )
    point_out, tap_out, gain_out, shift_out = call(
        functools.partial(unpack_kernel, pieces, batch),
        [("v", gathered)],
        [("v", (share, channels), F32), ("v", (9, share), F32), ("v", (share,), F32), ("v", (share,), F32)],
        [pltpu.VMEM((total, channels), F32)],
    )
    return (
        block_out.reshape(inputs.shape),
        grad_input.reshape(inputs.shape),
        point_out.T,
        tap_out,
        gain_out,
        shift_out,
    )


def solution(mesh):
    return jax.shard_map(
        local,
        mesh=mesh,
        in_specs=(
            P("dp", "slab", None),
            P("dp", "slab", None),
            P("dp", "slab", None),
            P(),
            P(),
            P(),
            P(),
            P(),
        ),
        out_specs=(
            P("dp", "slab", None),
            P("dp", "slab", None),
            P(None, "slab"),
            P(None, "slab"),
            P("slab"),
            P("slab"),
        ),
        check_vma=False,
    )
```

```python
import functools

import jax
import jax.numpy as jnp
from jax import lax
from jax.experimental import pallas as pl
from jax.experimental.pallas import tpu as pltpu
from jax.sharding import PartitionSpec as P

F32 = jnp.float32
BF16 = jnp.bfloat16
LANES = 128
SUB = 8
EPS = 1e-05
DMA = pltpu.SemaphoreType.DMA


def round_up(value, unit):
    return -(-value // unit) * unit


def tiles(width):
    return [(start, min(LANES, width - start)) for start in range(0, width, LANES)]


def column(ref, col, channels, scale=None):
    start = col * channels
    base = start // LANES * LANES
    off = start - base
    end = min(ref.shape[1], base + round_up(off + channels, LANES))
    values = ref[:, base:end].astype(F32)
    if scale is not None:
        values = values * jnp.concatenate([scale] * ((end - base) // LANES), axis=1)
    return values[:, off : off + channels]


def pixel_weights(class_ref, label_ref):
    labels = jnp.concatenate([label_ref[r] for r in range(label_ref.shape[0])], axis=0)
    weight = jnp.zeros(labels.shape, F32)
    for t in range(class_ref.shape[0]):
        weight = jnp.where(labels == t, class_ref[t], weight)
    return weight


def spread_weights(ref, weight):
    for col in range(ref.shape[0]):
        ref[col] = jnp.broadcast_to(weight[:, col : col + 1], ref.shape[1:])


def fetches(sources, buffers, sems):
    copies = [pltpu.make_async_copy(s, b, sems.at[i]) for i, (s, b) in enumerate(zip(sources, buffers))]
    for copy in copies:
        copy.start()
    return copies


def prepare_kernel(class_ref, x_ref, u_ref, label_ref, kernel_ref, active_ref, part_ref, grad_ref, class_buf, x_buf, u_buf, label_buf, kernel_buf, weight_buf, sems):
    rows, _, cols = label_buf.shape
    sub, channels = grad_ref.shape[1:]
    got_x, got_kernel, got_u, got_label, got_class = fetches(
        (x_ref.at[0], kernel_ref, u_ref.at[0], label_ref, class_ref), (x_buf, kernel_buf, u_buf, label_buf, class_buf), sems
    )
    below = jnp.zeros((sub - rows, channels), F32)
    got_x.wait()
    for col in range(cols):
        active_ref[col] = jnp.concatenate([jnp.maximum(column(x_buf, col, channels), 0.0), below], axis=0)
    got_kernel.wait()
    for start, width in tiles(channels):
        at = pl.ds(start, width)
        taps = [kernel_buf[t : t + 1, at].astype(F32) for t in range(9)]
        before = jnp.zeros((sub, width), F32)
        pending = before
        for col in range(cols):
            mid = active_ref[col, :, at]
            up = pltpu.roll(mid, 1, 0)
            down = pltpu.roll(mid, sub - 1, 0)
            sums = [taps[j] * up + taps[3 + j] * mid + taps[6 + j] * down for j in range(3)]
            if col:
                part_ref[col - 1, :, at] = pending + sums[2]
            pending = before + sums[1]
            before = sums[0]
        part_ref[cols - 1, :, at] = pending
    got_u.wait()
    got_label.wait()
    got_class.wait()
    spread_weights(weight_buf, pixel_weights(class_buf, label_buf))
    for col in range(cols):
        grad_ref[col] = jnp.concatenate([column(u_buf, col, channels, weight_buf[col]), below], axis=0)


def forward_kernel(pieces, rows, where_ref, part_ref, own_ref, one_ref, two_ref, kernel_ref, point_ref, grad_ref, depth_ref, proj_ref, active_ref, stats_ref, part_buf, halo_buf, line_buf):
    cols, sub, channels = part_buf.shape
    even = where_ref[0] % 2 == 0
    near_line = jnp.where(even, rows, sub - 1)
    far_line = jnp.where(even, sub - 1, rows)
    far_line = jnp.where((where_ref[0] == 0) | (where_ref[0] == pieces - 1), sub, far_line)
    line_buf[...] = two_ref[...].astype(F32)
    for col in range(cols):
        start = col * channels
        base = start // LANES * LANES
        off = start - base
        end = min(one_ref.shape[2], base + round_up(off + channels, LANES))
        near = one_ref[0, :, base:end].astype(F32)
        one = jnp.where(even, near[:1], near[rows - 1 :])
        parts = [line_buf[t : t + 1, :] for t in range(base // LANES, -(-end // LANES))]
        two = jnp.concatenate(parts, axis=1)[:, : end - base]
        line = lax.broadcasted_iota(jnp.int32, (sub, end - base), 0)
        lines = jnp.maximum(jnp.where(line == near_line, one, jnp.where(line == far_line, two, 0.0)), 0.0)
        halo_buf[col] = lines[:, off : off + channels]
    line = lax.broadcasted_iota(jnp.int32, (sub, channels), 0)
    wide = [
        jnp.where(line == sub - 1, kernel_ref[j : j + 1, :].astype(F32), kernel_ref[6 + j : 7 + j, :].astype(F32))
        for j in range(3)
    ]
    for start, width in tiles(channels):
        at = pl.ds(start, width)
        row = lax.broadcasted_iota(jnp.int32, (sub, width), 0)
        taps = [w[:, start : start + width] for w in wide]

        def finish(col, value):
            shifted = jnp.where(row == 0, pltpu.roll(value, 1, 0), jnp.where(row == rows - 1, pltpu.roll(value, sub - 1, 0), 0.0))
            total = part_ref[col, :, at] + shifted
            part_buf[col, :, at] = jnp.where(row < rows, total, 0.0)

        before = jnp.zeros((sub, width), F32)
        pending = before
        for col in range(cols):
            halo = halo_buf[col, :, at]
            active_ref[col, :, at] = own_ref[col, :, at] + halo
            if col:
                finish(col - 1, pending + taps[2] * halo)
            pending = before + taps[1] * halo
            before = taps[0] * halo
        finish(cols - 1, pending)
    depth = part_buf[...].reshape(cols * sub, channels).astype(BF16)
    depth_ref[:, :channels] = depth
    depth_ref[:, channels:] = jnp.zeros((cols * sub, depth_ref.shape[1] - channels), BF16)
    proj_ref[...] = jnp.dot(depth, point_ref[...], preferred_element_type=F32)
    count = rows * cols
    for start, width in tiles(channels):
        at = pl.ds(start, width)
        proj = proj_ref[:, at]
        grads = grad_ref[:, :, at].reshape(cols * sub, width)
        mine = lax.broadcasted_iota(jnp.int32, (cols * sub, width), 0) % sub < rows
        center = jnp.sum(proj, axis=0, keepdims=True) / count
        deviation = jnp.where(mine, proj - center, 0.0)
        stats_ref[0:1, at] = center
        stats_ref[1:2, at] = jnp.sum(deviation * deviation, axis=0, keepdims=True)
        stats_ref[2:3, at] = jnp.sum(grads, axis=0, keepdims=True)
        stats_ref[3:4, at] = jnp.sum(grads * deviation, axis=0, keepdims=True)
        stats_ref[4:SUB, at] = jnp.zeros((SUB - 4, width), F32)


def paired_sum(values):
    while len(values) > 1:
        values = [sum(values[i : i + 2]) for i in range(0, len(values), 2)]
    return values[0]


def cotangent_kernel(pieces, rows, proj_ref, grad_ref, gain_ref, *refs):
    stats_refs, (full_ref, norm_ref) = refs[:-2], refs[-2:]
    cols, sub, channels = grad_ref.shape
    local = rows * cols
    count = local * pieces
    stats = [ref[p : p + 4, :] for ref in stats_refs for p in range(0, ref.shape[0], SUB)]
    center = paired_sum([s[0:1] for s in stats]) / pieces
    square = paired_sum([s[1:2] + local * (s[0:1] - center) ** 2 for s in stats])
    shift_part = paired_sum([s[2:3] for s in stats])
    cross = paired_sum([s[3:4] + (s[0:1] - center) * s[2:3] for s in stats])
    inverse = lax.rsqrt(square / count + EPS)
    gain_part = cross * inverse
    gain = gain_ref[...].reshape(1, channels)
    norm_ref[0:1, :] = center
    norm_ref[1:2, :] = inverse
    norm_ref[2:3, :] = gain_part
    norm_ref[3:4, :] = shift_part
    norm_ref[4:SUB, :] = jnp.zeros((SUB - 4, channels), F32)
    for start, width in tiles(channels):
        at = slice(start, start + width)
        mine = lax.broadcasted_iota(jnp.int32, (cols * sub, width), 0) % sub < rows
        normed = (proj_ref[:, start : start + width] - center[:, at]) * inverse[:, at]
        grads = grad_ref[:, :, start : start + width].reshape(cols * sub, width)
        value = (gain * inverse)[:, at] * (grads - (shift_part / count)[:, at] - normed * (gain_part / count)[:, at])
        full_ref[:, start : start + width] = jnp.where(mine, value, 0.0).astype(BF16)
    full_ref[:, channels:] = jnp.zeros((cols * sub, full_ref.shape[1] - channels), BF16)


def product_kernel(full_ref, depth_ref, out_ref):
    channels = out_ref.shape[1]
    out_ref[...] = lax.dot_general(
        full_ref[:, :channels], depth_ref[:, :channels], (((0,), (0,)), ((), ())), preferred_element_type=F32
    )


def shares_kernel(pieces, share, where_ref, full_ref, depth_ref, own_ref, *refs):
    outs, total_ref = refs[:-1], refs[-1]
    product_kernel(full_ref, depth_ref, total_ref)
    for owner in range(pieces):

        @pl.when(where_ref[0] == owner)
        def _():
            def part(place):
                at = slice(place * share, (place + 1) * share)
                return total_ref[at, :] + own_ref[at, :]

            if pieces == 4:
                keep_ref, send_ref = outs
                keep_ref[...] = part(owner)
                send_ref[...] = part(owner ^ 2).astype(BF16)
            else:
                for j in range(pieces // 2):
                    outs[0][j] = part(2 * j + owner % 2)


def backward_kernel(rows, where_ref, full_ref, point_ref, active_ref, depth_grad_ref, tap_ref, one_ref, two_ref, point_buf, active_buf, grad_buf, sems):
    cols, sub, channels = active_buf.shape
    got_point, got_active = fetches((point_ref, active_ref), (point_buf, active_buf), sems)
    put = pltpu.make_async_copy(grad_buf, depth_grad_ref, sems.at[2])
    got_point.wait()
    grad = lax.dot_general(full_ref[:, :channels], point_buf[...], (((1,), (1,)), ((), ())), preferred_element_type=F32)
    grad_buf[...] = grad.astype(BF16).astype(F32).reshape(cols, sub, channels)
    put.start()
    even = where_ref[0] % 2 == 0
    first = grad_buf[:, 0, :].astype(BF16)
    last = grad_buf[:, rows - 1, :].astype(BF16)
    one_ref[...] = jnp.where(even, last, first)
    two_ref[...] = jnp.where(even, first, last)
    got_active.wait()
    for start, width in tiles(channels):
        at = pl.ds(start, width)
        totals = [jnp.zeros((sub, width), F32) for _ in range(9)]
        zero = jnp.zeros((sub, width), F32)
        ahead = grad_buf[0, :, at]
        here = zero
        for col in range(cols):
            behind, here = here, ahead
            ahead = grad_buf[col + 1, :, at] if col + 1 < cols else zero
            mid = active_buf[col, :, at]
            shifted = (pltpu.roll(mid, 1, 0), mid, pltpu.roll(mid, sub - 1, 0))
            for i in range(3):
                for j, other in enumerate((ahead, here, behind)):
                    totals[3 * i + j] = totals[3 * i + j] + shifted[i] * other
        for t in range(9):
            tap_ref[t : t + 1, at] = jnp.sum(totals[t], axis=0, keepdims=True)
        tap_ref[9:, at] = jnp.zeros((tap_ref.shape[0] - 9, width), F32)
    put.wait()


def fold(small, pieces, owner):
    share = small.shape[1] // pieces
    lines = -(-small.shape[0] // pieces)
    mine = small[:, owner * share : (owner + 1) * share]
    spare = lines * pieces - small.shape[0]
    if spare:
        mine = jnp.concatenate([mine, jnp.zeros((spare, share), F32)], axis=0)
    return jnp.concatenate([mine[q * lines : (q + 1) * lines] for q in range(pieces)], axis=1)


def unfold(lines, pieces, count):
    share = lines.shape[1] // pieces
    return jnp.concatenate([lines[:, q * share : (q + 1) * share] for q in range(pieces)], axis=0)[:count]


def store_halves(ref, start, lines):
    count = lines.shape[0]
    high = lines.astype(BF16).astype(F32)
    ref[start : start + count, :] = high
    ref[start + count : start + 2 * count, :] = lines - high


def small_kernel(pieces, where_ref, taps_ref, other_ref, norm_ref, stay_ref, leave_ref):
    taps = taps_ref[:9, :] + other_ref[:9, :]
    group = norm_ref[2:4, :]
    stay = jnp.concatenate([taps, group], axis=0)
    leave = jnp.concatenate([taps, jnp.zeros_like(group)], axis=0)
    for owner in range(pieces):

        @pl.when(where_ref[0] == owner)
        def _():
            stay_ref[...] = fold(stay, pieces, owner)
            leave_ref[...] = fold(leave, pieces, owner ^ 2)


def fold_kernel(pieces, where_ref, taps_ref, norm_ref, stay_ref, leave_ref):
    step = taps_ref.shape[0] // pieces
    taps = sum(taps_ref[p * step : p * step + 9, :] for p in range(pieces))
    small = jnp.concatenate([taps, norm_ref[2:4, :]], axis=0)
    for owner in range(pieces):

        @pl.when(where_ref[0] == owner)
        def _():
            stay_ref[...] = fold(small, pieces, owner)

    leave_ref[...] = jnp.zeros(leave_ref.shape, F32)


def pack_kernel(keep_ref, came_ref, fold_ref, other_ref, out_ref, flat_ref):
    copies, piece, channels = out_ref.shape
    share, lines = keep_ref.shape[0], fold_ref.shape[0]
    flat_ref[:share, :] = keep_ref[...] + came_ref[...].astype(F32)
    store_halves(flat_ref, share, fold_ref[...] + other_ref[...])
    rest = flat_ref.shape[0] - share - 2 * lines
    if rest:
        flat_ref[share + 2 * lines :, :] = jnp.zeros((rest, channels), F32)
    for k in range(copies):
        out_ref[k] = flat_ref[k * piece : (k + 1) * piece, :].astype(BF16)


def total_kernel(in_ref, out_ref):
    copies = in_ref.shape[0]
    total = in_ref[0].astype(F32)
    for k in range(1, copies):
        total = total + in_ref[k].astype(F32)
    total = total.astype(BF16)
    for k in range(copies):
        out_ref[k] = total


def unpack_kernel(pieces, batch, *refs):
    ins, (point_ref, tap_ref, gain_ref, shift_ref, flat_ref) = refs[:-5], refs[-5:]
    share = point_ref.shape[0]
    start = 0
    for in_ref in ins:
        copies, piece, _ = in_ref.shape
        for k in range(copies):
            flat_ref[start : start + piece, :] = in_ref[k].astype(F32) / batch
            start += piece
    point_ref[...] = flat_ref[:share, :]
    lines = -(-11 // pieces)
    total = flat_ref[share : share + lines, :] + flat_ref[share + lines : share + 2 * lines, :]
    small = unfold(total, pieces, 11)
    tap_ref[...] = small[:9]
    gain_ref[...] = small[9:10].reshape(share)
    shift_ref[...] = small[10:11].reshape(share)


def block_kernel(rows, x_ref, proj_ref, norm_ref, gain_ref, shift_ref, block_ref, x_buf, proj_buf, flat_ref, sems):
    channels = proj_buf.shape[1]
    cols = flat_ref.shape[1] // channels
    sub = proj_buf.shape[0] // cols
    got_x, got_proj = fetches((x_ref.at[0], proj_ref), (x_buf, proj_buf), sems)
    center, inverse = norm_ref[0:1, :], norm_ref[1:2, :]
    gain, shift = gain_ref[...].reshape(1, channels), shift_ref[...].reshape(1, channels)
    got_x.wait()
    got_proj.wait()
    for col in range(cols):
        normed = (proj_buf[col * sub : col * sub + rows, :] - center) * inverse
        result = column(x_buf, col, channels) + gain * normed + shift
        flat_ref[:, col * channels : (col + 1) * channels] = result
    block_ref[...] = flat_ref[...].astype(BF16)


def input_kernel(pieces, rows, where_ref, class_ref, x_ref, u_ref, label_ref, depth_grad_ref, one_ref, two_ref, kernel_ref, input_ref, x_buf, u_buf, halo_buf, flat_ref, class_buf, label_buf, kernel_buf, weight_buf, sems):
    cols, sub, channels = halo_buf.shape
    got_grad, got_kernel, got_x, got_u, got_label, got_class = fetches(
        (depth_grad_ref, kernel_ref, x_ref.at[0], u_ref.at[0], label_ref, class_ref),
        (halo_buf, kernel_buf, x_buf, u_buf, label_buf, class_buf),
        sems,
    )
    even = where_ref[0] % 2 == 0
    has_top = jnp.where(where_ref[0] > 0, 1.0, 0.0)
    has_bottom = jnp.where(where_ref[0] < pieces - 1, 1.0, 0.0)
    one = one_ref[...].astype(F32)
    two = two_ref[...].astype(F32)
    top = jnp.where(even, two, one) * has_top
    bottom = jnp.where(even, one, two) * has_bottom
    line = lax.broadcasted_iota(jnp.int32, (sub, channels), 0)
    got_grad.wait()
    got_kernel.wait()
    for col in range(cols):
        halo_buf[col] = jnp.where(
            line == rows, bottom[col : col + 1], jnp.where(line == sub - 1, top[col : col + 1], halo_buf[col])
        )
    for start, width in tiles(channels):
        at = pl.ds(start, width)
        taps = [kernel_buf[t : t + 1, at].astype(F32) for t in range(9)]
        before = jnp.zeros((sub, width), F32)
        pending = before
        for col in range(cols):
            mid = halo_buf[col, :, at]
            up = pltpu.roll(mid, 1, 0)
            down = pltpu.roll(mid, sub - 1, 0)
            sums = [taps[j] * down + taps[3 + j] * mid + taps[6 + j] * up for j in range(3)]
            if col:
                halo_buf[col - 1, :, at] = pending + sums[0]
            pending = before + sums[1]
            before = sums[2]
        halo_buf[cols - 1, :, at] = pending
    got_x.wait()
    got_u.wait()
    got_label.wait()
    got_class.wait()
    spread_weights(weight_buf, pixel_weights(class_buf, label_buf))
    for col in range(cols):
        grads = column(u_buf, col, channels, weight_buf[col])
        image = column(x_buf, col, channels)
        flat_ref[:, col * channels : (col + 1) * channels] = grads + jnp.where(image > 0, halo_buf[col, :rows, :], 0.0)
    input_ref[...] = flat_ref[...].astype(BF16)


def call(body, ins, outs, scratch=(), megabytes=16):
    space = {
        "o": pl.BlockSpec(memory_space=pl.ANY),
        "v": pl.BlockSpec(memory_space=pltpu.VMEM),
        "s": pl.BlockSpec(memory_space=pltpu.SMEM),
        "a": pl.BlockSpec(memory_space=pl.ANY),
    }
    return pl.pallas_call(
        body,
        out_shape=[pltpu.HBM(shape, dtype) if s == "a" else jax.ShapeDtypeStruct(shape, dtype) for s, shape, dtype in outs],
        in_specs=[space[s] for s, _ in ins],
        out_specs=[space[s] for s, _, _ in outs],
        scratch_shapes=list(scratch),
        compiler_params=pltpu.CompilerParams(vmem_limit_bytes=megabytes * 1024 * 1024),
    )(*[pltpu.with_memory_space_constraint(a, pltpu.HBM) if s == "a" else a for s, a in ins])


def local(inputs, upstream, labels, class_weights, depth_kernel, point_weight, gain, shift):
    samples, rows, flat = inputs.shape
    assert samples == 1
    channels = point_weight.shape[0]
    cols = flat // channels
    pieces = lax.axis_size("slab")
    copies = lax.axis_size("dp")
    assert pieces % 2 == 0
    share = channels // pieces
    sub = round_up(rows + 2, SUB)
    padded = round_up(channels, LANES)
    me = lax.axis_index("slab")
    where = me.astype(jnp.int32).reshape(1)
    even = me % 2 == 0
    image = inputs.reshape(rows, flat)
    near = [(i, i ^ 1) for i in range(pieces)]
    far = [(i, (i - 1) % pieces if i % 2 == 0 else (i + 1) % pieces) for i in range(pieces)]
    lane3 = (cols, sub, channels)
    pixels = cols * sub
    buf3 = pltpu.VMEM(lane3, F32)
    flat_buf = pltpu.VMEM((rows, flat), BF16)
    flat_f32 = pltpu.VMEM((rows, flat), F32)
    point_buf = pltpu.VMEM((channels, channels), BF16)
    kernel_buf = pltpu.VMEM(depth_kernel.shape, BF16)
    label_buf = pltpu.VMEM((rows, 1, cols), labels.dtype)
    label_lines = jnp.transpose(labels, (1, 0, 2))
    weight_buf = pltpu.VMEM((cols, rows, LANES), F32)
    class_buf = pltpu.SMEM(class_weights.shape, F32)

    one = lax.ppermute(inputs, "slab", near)
    edge = lax.dynamic_slice_in_dim(image, jnp.where(even, 0, rows - 1), 1, 0)[0]
    two = lax.ppermute(jnp.pad(edge, (0, -flat % LANES)).reshape(-1, LANES), "slab", far)
    own, part, grad_out = call(
        prepare_kernel,
        [("a", class_weights), ("a", inputs), ("a", upstream), ("a", label_lines), ("a", depth_kernel)],
        [("v", lane3, F32), ("v", lane3, F32), ("v", lane3, F32)],
        [class_buf, flat_buf, flat_buf, label_buf, kernel_buf, weight_buf, DMA((5,))],
        megabytes=16,
    )
    depth, projected, active, stats = call(
        functools.partial(forward_kernel, pieces, rows),
        [("s", where), ("v", part), ("v", own), ("v", one), ("v", two), ("v", depth_kernel), ("v", point_weight), ("v", grad_out)],
        [("v", (pixels, padded), BF16), ("v", (pixels, channels), F32), ("v", lane3, F32), ("v", (SUB, channels), F32)],
        [buf3, buf3, pltpu.VMEM(two.shape, F32)],
    )
    other_depth = lax.ppermute(depth, "slab", near)
    across = [(i, i ^ 2) for i in range(pieces)]
    if pieces == 4:
        apart = [(i, i ^ 3) for i in range(pieces)]
        all_stats = [stats, *(lax.ppermute(stats, "slab", pairs) for pairs in (near, across, apart))]
    else:
        all_stats = [lax.all_gather(stats, "slab", axis=0, tiled=True)]
    full, norm = call(
        functools.partial(cotangent_kernel, pieces, rows),
        [("v", projected), ("v", grad_out), ("v", gain), *(("v", part) for part in all_stats)],
        [("v", (pixels, padded), BF16), ("v", (SUB, channels), F32)],
    )
    theirs = lax.ppermute(full, "slab", near)
    (own_product,) = call(product_kernel, [("v", full), ("v", depth)], [("v", (channels, channels), F32)])
    lines = -(-11 // pieces)
    batch = samples * copies
    if pieces == 4:
        share_outs = [("v", (share, channels), F32), ("v", (share, channels), BF16)]
    else:
        share_outs = [("v", (pieces // 2, share, channels), F32)]
    products = call(
        functools.partial(shares_kernel, pieces, share),
        [("s", where), ("v", theirs), ("v", other_depth), ("v", own_product)],
        share_outs,
        [pltpu.VMEM((channels, channels), F32)],
    )
    if pieces == 4:
        keep, leaving = products
    else:
        blocks = products[0]
        while blocks.shape[0] > 2:
            half = blocks.shape[0] // 2
            high = ((me // 2) & half) != 0
            mine = lax.dynamic_slice_in_dim(blocks, jnp.where(high, half, 0), half, 0)
            leaving = lax.dynamic_slice_in_dim(blocks, jnp.where(high, 0, half), half, 0).astype(BF16)
            came = lax.ppermute(leaving, "slab", [(i, i ^ (2 * half)) for i in range(pieces)])
            blocks = mine + came.astype(F32)
        bit = (me // 2) % 2
        keep = blocks[0] if pieces == 2 else lax.dynamic_index_in_dim(blocks, bit, 0, False)
        leaving = None if pieces == 2 else lax.dynamic_index_in_dim(blocks, 1 - bit, 0, False).astype(BF16)
    if pieces > 2:
        leaving, full = lax.optimization_barrier((leaving, full))
        came = lax.ppermute(leaving, "slab", across)
    else:
        came = jnp.zeros((share, channels), BF16)
    depth_grad, taps, edge_one, edge_two = call(
        functools.partial(backward_kernel, rows),
        [("s", where), ("v", full), ("o", point_weight), ("o", active)],
        [("a", lane3, F32), ("v", (2 * SUB, channels), F32), ("v", (cols, channels), BF16), ("v", (cols, channels), BF16)],
        [point_buf, buf3, buf3, DMA((3,))],
    )
    fold_outs = [("v", (lines, channels), F32)] * 2
    if pieces == 4:
        stay, leave = call(
            functools.partial(small_kernel, pieces),
            [("s", where), ("v", taps), ("v", lax.ppermute(taps, "slab", near)), ("v", norm)],
            fold_outs,
        )
        leave, norm = lax.optimization_barrier((leave, norm))
        leave = lax.ppermute(leave, "slab", across)
    else:
        all_taps = lax.all_gather(taps, "slab", axis=0, tiled=True)
        stay, leave = call(functools.partial(fold_kernel, pieces), [("s", where), ("v", all_taps), ("v", norm)], fold_outs)
    (block_out,) = call(
        functools.partial(block_kernel, rows),
        [("a", inputs), ("o", projected), ("v", norm), ("v", gain), ("v", shift)],
        [("v", (rows, flat), BF16)],
        [flat_buf, pltpu.VMEM((pixels, channels), F32), flat_f32, DMA((2,))],
    )
    stay, block_out = lax.optimization_barrier((stay, block_out))
    piece = -(-(share + 2 * lines) // copies)
    total = piece * copies
    (packed,) = call(
        pack_kernel,
        [("v", keep), ("v", came), ("v", stay), ("v", leave)],
        [("v", (copies, piece, channels), BF16)],
        [pltpu.VMEM((total, channels), F32)],
    )
    landed = lax.all_to_all(packed, "dp", 0, 0)
    (summed,) = call(total_kernel, [("v", landed)], [("v", packed.shape, BF16)])
    gathered = lax.all_to_all(summed, "dp", 0, 0)
    halo_one = lax.ppermute(edge_one, "slab", near)
    halo_two = lax.ppermute(edge_two, "slab", far)
    (grad_input,) = call(
        functools.partial(input_kernel, pieces, rows),
        [("s", where), ("a", class_weights), ("a", inputs), ("a", upstream), ("a", label_lines), ("a", depth_grad), ("v", halo_one), ("v", halo_two), ("a", depth_kernel)],
        [("v", (rows, flat), BF16)],
        [flat_buf, flat_buf, buf3, flat_f32, class_buf, label_buf, kernel_buf, weight_buf, DMA((6,))],
    )
    point_out, tap_out, gain_out, shift_out = call(
        functools.partial(unpack_kernel, pieces, batch),
        [("v", gathered)],
        [("v", (share, channels), F32), ("v", (9, share), F32), ("v", (share,), F32), ("v", (share,), F32)],
        [pltpu.VMEM((total, channels), F32)],
    )
    return (
        block_out.reshape(inputs.shape),
        grad_input.reshape(inputs.shape),
        point_out.T,
        tap_out,
        gain_out,
        shift_out,
    )


def solution(mesh):
    return jax.shard_map(
        local,
        mesh=mesh,
        in_specs=(
            P("dp", "slab", None),
            P("dp", "slab", None),
            P("dp", "slab", None),
            P(),
            P(),
            P(),
            P(),
            P(),
        ),
        out_specs=(
            P("dp", "slab", None),
            P("dp", "slab", None),
            P(None, "slab"),
            P(None, "slab"),
            P("slab"),
            P("slab"),
        ),
        check_vma=False,
    )
```

```python
import functools

import jax
import jax.numpy as jnp
from jax import lax
from jax.experimental import pallas as pl
from jax.experimental.pallas import tpu as pltpu
from jax.sharding import PartitionSpec as P

F32 = jnp.float32
BF16 = jnp.bfloat16
LANES = 128
SUB = 8
EPS = 1e-05
DMA = pltpu.SemaphoreType.DMA


def round_up(value, unit):
    return -(-value // unit) * unit


def tiles(width):
    return [(start, min(LANES, width - start)) for start in range(0, width, LANES)]


def column(ref, col, channels, scale=None):
    start = col * channels
    base = start // LANES * LANES
    off = start - base
    end = min(ref.shape[1], base + round_up(off + channels, LANES))
    values = ref[:, base:end].astype(F32)
    if scale is not None:
        values = values * jnp.concatenate([scale] * ((end - base) // LANES), axis=1)
    return values[:, off : off + channels]


def pixel_weights(class_ref, label_ref):
    labels = jnp.concatenate([label_ref[r] for r in range(label_ref.shape[0])], axis=0)
    weight = jnp.zeros(labels.shape, F32)
    for t in range(class_ref.shape[0]):
        weight = jnp.where(labels == t, class_ref[t], weight)
    return weight


def spread_weights(ref, weight):
    for col in range(ref.shape[0]):
        ref[col] = jnp.broadcast_to(weight[:, col : col + 1], ref.shape[1:])


def fetches(sources, buffers, sems):
    copies = [pltpu.make_async_copy(s, b, sems.at[i]) for i, (s, b) in enumerate(zip(sources, buffers))]
    for copy in copies:
        copy.start()
    return copies


def prepare_kernel(class_ref, x_ref, u_ref, label_ref, kernel_ref, active_ref, part_ref, grad_ref, class_buf, x_buf, u_buf, label_buf, kernel_buf, weight_buf, sems):
    rows, _, cols = label_buf.shape
    sub, channels = grad_ref.shape[1:]
    got_x, got_kernel, got_u, got_label, got_class = fetches(
        (x_ref.at[0], kernel_ref, u_ref.at[0], label_ref, class_ref), (x_buf, kernel_buf, u_buf, label_buf, class_buf), sems
    )
    below = jnp.zeros((sub - rows, channels), F32)
    got_x.wait()
    for col in range(cols):
        active_ref[col] = jnp.concatenate([jnp.maximum(column(x_buf, col, channels), 0.0), below], axis=0)
    got_kernel.wait()
    for start, width in tiles(channels):
        at = pl.ds(start, width)
        taps = [kernel_buf[t : t + 1, at].astype(F32) for t in range(9)]
        before = jnp.zeros((sub, width), F32)
        pending = before
        for col in range(cols):
            mid = active_ref[col, :, at]
            up = pltpu.roll(mid, 1, 0)
            down = pltpu.roll(mid, sub - 1, 0)
            sums = [taps[j] * up + taps[3 + j] * mid + taps[6 + j] * down for j in range(3)]
            if col:
                part_ref[col - 1, :, at] = pending + sums[2]
            pending = before + sums[1]
            before = sums[0]
        part_ref[cols - 1, :, at] = pending
    got_u.wait()
    got_label.wait()
    got_class.wait()
    spread_weights(weight_buf, pixel_weights(class_buf, label_buf))
    for col in range(cols):
        grad_ref[col] = jnp.concatenate([column(u_buf, col, channels, weight_buf[col]), below], axis=0)


def forward_kernel(pieces, rows, where_ref, part_ref, own_ref, one_ref, two_ref, kernel_ref, point_ref, grad_ref, depth_ref, proj_ref, active_ref, stats_ref, part_buf, halo_buf, line_buf):
    cols, sub, channels = part_buf.shape
    even = where_ref[0] % 2 == 0
    near_line = jnp.where(even, rows, sub - 1)
    far_line = jnp.where(even, sub - 1, rows)
    far_line = jnp.where((where_ref[0] == 0) | (where_ref[0] == pieces - 1), sub, far_line)
    line_buf[...] = two_ref[...].astype(F32)
    for col in range(cols):
        start = col * channels
        base = start // LANES * LANES
        off = start - base
        end = min(one_ref.shape[2], base + round_up(off + channels, LANES))
        near = one_ref[0, :, base:end].astype(F32)
        one = jnp.where(even, near[:1], near[rows - 1 :])
        parts = [line_buf[t : t + 1, :] for t in range(base // LANES, -(-end // LANES))]
        two = jnp.concatenate(parts, axis=1)[:, : end - base]
        line = lax.broadcasted_iota(jnp.int32, (sub, end - base), 0)
        lines = jnp.maximum(jnp.where(line == near_line, one, jnp.where(line == far_line, two, 0.0)), 0.0)
        halo_buf[col] = lines[:, off : off + channels]
    line = lax.broadcasted_iota(jnp.int32, (sub, channels), 0)
    wide = [
        jnp.where(line == sub - 1, kernel_ref[j : j + 1, :].astype(F32), kernel_ref[6 + j : 7 + j, :].astype(F32))
        for j in range(3)
    ]
    for start, width in tiles(channels):
        at = pl.ds(start, width)
        row = lax.broadcasted_iota(jnp.int32, (sub, width), 0)
        taps = [w[:, start : start + width] for w in wide]

        def finish(col, value):
            shifted = jnp.where(row == 0, pltpu.roll(value, 1, 0), jnp.where(row == rows - 1, pltpu.roll(value, sub - 1, 0), 0.0))
            total = part_ref[col, :, at] + shifted
            part_buf[col, :, at] = jnp.where(row < rows, total, 0.0)

        before = jnp.zeros((sub, width), F32)
        pending = before
        for col in range(cols):
            halo = halo_buf[col, :, at]
            active_ref[col, :, at] = own_ref[col, :, at] + halo
            if col:
                finish(col - 1, pending + taps[2] * halo)
            pending = before + taps[1] * halo
            before = taps[0] * halo
        finish(cols - 1, pending)
    depth = part_buf[...].reshape(cols * sub, channels).astype(BF16)
    depth_ref[:, :channels] = depth
    depth_ref[:, channels:] = jnp.zeros((cols * sub, depth_ref.shape[1] - channels), BF16)
    proj_ref[...] = jnp.dot(depth, point_ref[...], preferred_element_type=F32)
    count = rows * cols
    for start, width in tiles(channels):
        at = pl.ds(start, width)
        proj = proj_ref[:, at]
        grads = grad_ref[:, :, at].reshape(cols * sub, width)
        mine = lax.broadcasted_iota(jnp.int32, (cols * sub, width), 0) % sub < rows
        center = jnp.sum(proj, axis=0, keepdims=True) / count
        deviation = jnp.where(mine, proj - center, 0.0)
        stats_ref[0:1, at] = center
        stats_ref[1:2, at] = jnp.sum(deviation * deviation, axis=0, keepdims=True)
        stats_ref[2:3, at] = jnp.sum(grads, axis=0, keepdims=True)
        stats_ref[3:4, at] = jnp.sum(grads * deviation, axis=0, keepdims=True)
        stats_ref[4:SUB, at] = jnp.zeros((SUB - 4, width), F32)


def paired_sum(values):
    while len(values) > 1:
        values = [sum(values[i : i + 2]) for i in range(0, len(values), 2)]
    return values[0]


def cotangent_kernel(pieces, rows, proj_ref, grad_ref, gain_ref, *refs):
    stats_refs, (full_ref, norm_ref) = refs[:-2], refs[-2:]
    cols, sub, channels = grad_ref.shape
    local = rows * cols
    count = local * pieces
    stats = [ref[p : p + 4, :] for ref in stats_refs for p in range(0, ref.shape[0], SUB)]
    center = paired_sum([s[0:1] for s in stats]) / pieces
    square = paired_sum([s[1:2] + local * (s[0:1] - center) ** 2 for s in stats])
    shift_part = paired_sum([s[2:3] for s in stats])
    cross = paired_sum([s[3:4] + (s[0:1] - center) * s[2:3] for s in stats])
    inverse = lax.rsqrt(square / count + EPS)
    gain_part = cross * inverse
    gain = gain_ref[...].reshape(1, channels)
    norm_ref[0:1, :] = center
    norm_ref[1:2, :] = inverse
    norm_ref[2:3, :] = gain_part
    norm_ref[3:4, :] = shift_part
    norm_ref[4:SUB, :] = jnp.zeros((SUB - 4, channels), F32)
    for start, width in tiles(channels):
        at = slice(start, start + width)
        mine = lax.broadcasted_iota(jnp.int32, (cols * sub, width), 0) % sub < rows
        normed = (proj_ref[:, start : start + width] - center[:, at]) * inverse[:, at]
        grads = grad_ref[:, :, start : start + width].reshape(cols * sub, width)
        value = (gain * inverse)[:, at] * (grads - (shift_part / count)[:, at] - normed * (gain_part / count)[:, at])
        full_ref[:, start : start + width] = jnp.where(mine, value, 0.0).astype(BF16)
    full_ref[:, channels:] = jnp.zeros((cols * sub, full_ref.shape[1] - channels), BF16)


def product_kernel(full_ref, depth_ref, out_ref):
    channels = out_ref.shape[1]
    out_ref[...] = lax.dot_general(
        full_ref[:, :channels], depth_ref[:, :channels], (((0,), (0,)), ((), ())), preferred_element_type=F32
    )


def shares_kernel(pieces, share, where_ref, full_ref, depth_ref, own_ref, *refs):
    outs, total_ref = refs[:-1], refs[-1]
    product_kernel(full_ref, depth_ref, total_ref)
    for owner in range(pieces):

        @pl.when(where_ref[0] == owner)
        def _():
            def part(place):
                at = slice(place * share, (place + 1) * share)
                return total_ref[at, :] + own_ref[at, :]

            if pieces == 4:
                keep_ref, send_ref = outs
                keep_ref[...] = part(owner)
                send_ref[...] = part(owner ^ 2).astype(BF16)
            else:
                for j in range(pieces // 2):
                    outs[0][j] = part(2 * j + owner % 2)


def backward_kernel(rows, where_ref, full_ref, point_ref, active_ref, depth_grad_ref, tap_ref, one_ref, two_ref, point_buf, active_buf, grad_buf, sems):
    cols, sub, channels = active_buf.shape
    got_point, got_active = fetches((point_ref, active_ref), (point_buf, active_buf), sems)
    put = pltpu.make_async_copy(grad_buf, depth_grad_ref, sems.at[2])
    got_point.wait()
    grad = lax.dot_general(full_ref[:, :channels], point_buf[...], (((1,), (1,)), ((), ())), preferred_element_type=F32)
    grad_buf[...] = grad.astype(BF16).astype(F32).reshape(cols, sub, channels)
    put.start()
    even = where_ref[0] % 2 == 0
    first = grad_buf[:, 0, :].astype(BF16)
    last = grad_buf[:, rows - 1, :].astype(BF16)
    one_ref[...] = jnp.where(even, last, first)
    two_ref[...] = jnp.where(even, first, last)
    got_active.wait()
    for start, width in tiles(channels):
        at = pl.ds(start, width)
        totals = [jnp.zeros((sub, width), F32) for _ in range(9)]
        zero = jnp.zeros((sub, width), F32)
        ahead = grad_buf[0, :, at]
        here = zero
        for col in range(cols):
            behind, here = here, ahead
            ahead = grad_buf[col + 1, :, at] if col + 1 < cols else zero
            mid = active_buf[col, :, at]
            shifted = (pltpu.roll(mid, 1, 0), mid, pltpu.roll(mid, sub - 1, 0))
            for i in range(3):
                for j, other in enumerate((ahead, here, behind)):
                    totals[3 * i + j] = totals[3 * i + j] + shifted[i] * other
        for t in range(9):
            tap_ref[t : t + 1, at] = jnp.sum(totals[t], axis=0, keepdims=True)
        tap_ref[9:, at] = jnp.zeros((tap_ref.shape[0] - 9, width), F32)
    put.wait()


def fold(small, pieces, owner):
    share = small.shape[1] // pieces
    lines = -(-small.shape[0] // pieces)
    mine = small[:, owner * share : (owner + 1) * share]
    spare = lines * pieces - small.shape[0]
    if spare:
        mine = jnp.concatenate([mine, jnp.zeros((spare, share), F32)], axis=0)
    return jnp.concatenate([mine[q * lines : (q + 1) * lines] for q in range(pieces)], axis=1)


def unfold(lines, pieces, count):
    share = lines.shape[1] // pieces
    return jnp.concatenate([lines[:, q * share : (q + 1) * share] for q in range(pieces)], axis=0)[:count]


def store_halves(ref, start, lines):
    count = lines.shape[0]
    high = lines.astype(BF16).astype(F32)
    ref[start : start + count, :] = high
    ref[start + count : start + 2 * count, :] = lines - high


def small_kernel(pieces, where_ref, taps_ref, other_ref, norm_ref, stay_ref, leave_ref):
    taps = taps_ref[:9, :] + other_ref[:9, :]
    group = norm_ref[2:4, :]
    stay = jnp.concatenate([taps, group], axis=0)
    leave = jnp.concatenate([taps, jnp.zeros_like(group)], axis=0)
    for owner in range(pieces):

        @pl.when(where_ref[0] == owner)
        def _():
            stay_ref[...] = fold(stay, pieces, owner)
            leave_ref[...] = fold(leave, pieces, owner ^ 2)


def fold_kernel(pieces, where_ref, taps_ref, norm_ref, stay_ref, leave_ref):
    step = taps_ref.shape[0] // pieces
    taps = sum(taps_ref[p * step : p * step + 9, :] for p in range(pieces))
    small = jnp.concatenate([taps, norm_ref[2:4, :]], axis=0)
    for owner in range(pieces):

        @pl.when(where_ref[0] == owner)
        def _():
            stay_ref[...] = fold(small, pieces, owner)

    leave_ref[...] = jnp.zeros(leave_ref.shape, F32)


def pack_kernel(keep_ref, came_ref, fold_ref, other_ref, out_ref, flat_ref):
    copies, piece, channels = out_ref.shape
    share, lines = keep_ref.shape[0], fold_ref.shape[0]
    flat_ref[:share, :] = keep_ref[...] + came_ref[...].astype(F32)
    store_halves(flat_ref, share, fold_ref[...] + other_ref[...])
    rest = flat_ref.shape[0] - share - 2 * lines
    if rest:
        flat_ref[share + 2 * lines :, :] = jnp.zeros((rest, channels), F32)
    for k in range(copies):
        out_ref[k] = flat_ref[k * piece : (k + 1) * piece, :].astype(BF16)


def total_kernel(in_ref, out_ref):
    copies = in_ref.shape[0]
    total = in_ref[0].astype(F32)
    for k in range(1, copies):
        total = total + in_ref[k].astype(F32)
    total = total.astype(BF16)
    for k in range(copies):
        out_ref[k] = total


def scaled(values, batch):
    return values * (1.0 / batch) if batch & (batch - 1) == 0 else values / batch


def unpack_kernel(pieces, batch, *refs):
    ins, (point_ref, tap_ref, gain_ref, shift_ref, flat_ref) = refs[:-5], refs[-5:]
    share = point_ref.shape[0]
    start = 0
    for in_ref in ins:
        copies, piece, _ = in_ref.shape
        for k in range(copies):
            flat_ref[start : start + piece, :] = scaled(in_ref[k].astype(F32), batch)
            start += piece
    point_ref[...] = flat_ref[:share, :]
    lines = -(-11 // pieces)
    total = flat_ref[share : share + lines, :] + flat_ref[share + lines : share + 2 * lines, :]
    small = unfold(total, pieces, 11)
    tap_ref[...] = small[:9]
    gain_ref[...] = small[9:10].reshape(share)
    shift_ref[...] = small[10:11].reshape(share)


def block_kernel(rows, x_ref, proj_ref, norm_ref, gain_ref, shift_ref, block_ref, x_buf, proj_buf, flat_ref, sems):
    channels = proj_buf.shape[1]
    cols = flat_ref.shape[1] // channels
    sub = proj_buf.shape[0] // cols
    got_x, got_proj = fetches((x_ref.at[0], proj_ref), (x_buf, proj_buf), sems)
    center, inverse = norm_ref[0:1, :], norm_ref[1:2, :]
    gain, shift = gain_ref[...].reshape(1, channels), shift_ref[...].reshape(1, channels)
    got_x.wait()
    got_proj.wait()
    for col in range(cols):
        normed = (proj_buf[col * sub : col * sub + rows, :] - center) * inverse
        result = column(x_buf, col, channels) + gain * normed + shift
        flat_ref[:, col * channels : (col + 1) * channels] = result
    block_ref[...] = flat_ref[...].astype(BF16)


def input_kernel(pieces, rows, where_ref, class_ref, x_ref, u_ref, label_ref, depth_grad_ref, one_ref, two_ref, kernel_ref, input_ref, x_buf, u_buf, halo_buf, flat_ref, class_buf, label_buf, kernel_buf, weight_buf, sems):
    cols, sub, channels = halo_buf.shape
    got_grad, got_kernel, got_x, got_u, got_label, got_class = fetches(
        (depth_grad_ref, kernel_ref, x_ref.at[0], u_ref.at[0], label_ref, class_ref),
        (halo_buf, kernel_buf, x_buf, u_buf, label_buf, class_buf),
        sems,
    )
    even = where_ref[0] % 2 == 0
    has_top = jnp.where(where_ref[0] > 0, 1.0, 0.0)
    has_bottom = jnp.where(where_ref[0] < pieces - 1, 1.0, 0.0)
    one = one_ref[...].astype(F32)
    two = two_ref[...].astype(F32)
    top = jnp.where(even, two, one) * has_top
    bottom = jnp.where(even, one, two) * has_bottom
    line = lax.broadcasted_iota(jnp.int32, (sub, channels), 0)
    got_grad.wait()
    got_kernel.wait()
    for col in range(cols):
        halo_buf[col] = jnp.where(
            line == rows, bottom[col : col + 1], jnp.where(line == sub - 1, top[col : col + 1], halo_buf[col])
        )
    for start, width in tiles(channels):
        at = pl.ds(start, width)
        taps = [kernel_buf[t : t + 1, at].astype(F32) for t in range(9)]
        before = jnp.zeros((sub, width), F32)
        pending = before
        for col in range(cols):
            mid = halo_buf[col, :, at]
            up = pltpu.roll(mid, 1, 0)
            down = pltpu.roll(mid, sub - 1, 0)
            sums = [taps[j] * down + taps[3 + j] * mid + taps[6 + j] * up for j in range(3)]
            if col:
                halo_buf[col - 1, :, at] = pending + sums[0]
            pending = before + sums[1]
            before = sums[2]
        halo_buf[cols - 1, :, at] = pending
    got_x.wait()
    got_u.wait()
    got_label.wait()
    got_class.wait()
    spread_weights(weight_buf, pixel_weights(class_buf, label_buf))
    for col in range(cols):
        grads = column(u_buf, col, channels, weight_buf[col])
        image = column(x_buf, col, channels)
        flat_ref[:, col * channels : (col + 1) * channels] = grads + jnp.where(image > 0, halo_buf[col, :rows, :], 0.0)
    input_ref[...] = flat_ref[...].astype(BF16)


def call(body, ins, outs, scratch=(), megabytes=16):
    space = {
        "o": pl.BlockSpec(memory_space=pl.ANY),
        "v": pl.BlockSpec(memory_space=pltpu.VMEM),
        "s": pl.BlockSpec(memory_space=pltpu.SMEM),
        "a": pl.BlockSpec(memory_space=pl.ANY),
    }
    return pl.pallas_call(
        body,
        out_shape=[pltpu.HBM(shape, dtype) if s == "a" else jax.ShapeDtypeStruct(shape, dtype) for s, shape, dtype in outs],
        in_specs=[space[s] for s, _ in ins],
        out_specs=[space[s] for s, _, _ in outs],
        scratch_shapes=list(scratch),
        compiler_params=pltpu.CompilerParams(vmem_limit_bytes=megabytes * 1024 * 1024),
    )(*[pltpu.with_memory_space_constraint(a, pltpu.HBM) if s == "a" else a for s, a in ins])


def local(inputs, upstream, labels, class_weights, depth_kernel, point_weight, gain, shift):
    samples, rows, flat = inputs.shape
    assert samples == 1
    channels = point_weight.shape[0]
    cols = flat // channels
    pieces = lax.axis_size("slab")
    copies = lax.axis_size("dp")
    assert pieces % 2 == 0
    share = channels // pieces
    sub = round_up(rows + 2, SUB)
    padded = round_up(channels, LANES)
    me = lax.axis_index("slab")
    where = me.astype(jnp.int32).reshape(1)
    even = me % 2 == 0
    image = inputs.reshape(rows, flat)
    near = [(i, i ^ 1) for i in range(pieces)]
    far = [(i, (i - 1) % pieces if i % 2 == 0 else (i + 1) % pieces) for i in range(pieces)]
    lane3 = (cols, sub, channels)
    pixels = cols * sub
    buf3 = pltpu.VMEM(lane3, F32)
    flat_buf = pltpu.VMEM((rows, flat), BF16)
    flat_f32 = pltpu.VMEM((rows, flat), F32)
    point_buf = pltpu.VMEM((channels, channels), BF16)
    kernel_buf = pltpu.VMEM(depth_kernel.shape, BF16)
    label_buf = pltpu.VMEM((rows, 1, cols), labels.dtype)
    label_lines = jnp.transpose(labels, (1, 0, 2))
    weight_buf = pltpu.VMEM((cols, rows, LANES), F32)
    class_buf = pltpu.SMEM(class_weights.shape, F32)

    one = lax.ppermute(inputs, "slab", near)
    edge = lax.dynamic_slice_in_dim(image, jnp.where(even, 0, rows - 1), 1, 0)[0]
    two = lax.ppermute(jnp.pad(edge, (0, -flat % LANES)).reshape(-1, LANES), "slab", far)
    own, part, grad_out = call(
        prepare_kernel,
        [("a", class_weights), ("a", inputs), ("a", upstream), ("a", label_lines), ("a", depth_kernel)],
        [("v", lane3, F32), ("v", lane3, F32), ("v", lane3, F32)],
        [class_buf, flat_buf, flat_buf, label_buf, kernel_buf, weight_buf, DMA((5,))],
        megabytes=16,
    )
    depth, projected, active, stats = call(
        functools.partial(forward_kernel, pieces, rows),
        [("s", where), ("v", part), ("v", own), ("v", one), ("v", two), ("v", depth_kernel), ("v", point_weight), ("v", grad_out)],
        [("v", (pixels, padded), BF16), ("v", (pixels, channels), F32), ("v", lane3, F32), ("v", (SUB, channels), F32)],
        [buf3, buf3, pltpu.VMEM(two.shape, F32)],
    )
    other_depth = lax.ppermute(depth, "slab", near)
    across = [(i, i ^ 2) for i in range(pieces)]
    if pieces == 4:
        apart = [(i, i ^ 3) for i in range(pieces)]
        all_stats = [stats, *(lax.ppermute(stats, "slab", pairs) for pairs in (near, across, apart))]
    else:
        all_stats = [lax.all_gather(stats, "slab", axis=0, tiled=True)]
    full, norm = call(
        functools.partial(cotangent_kernel, pieces, rows),
        [("v", projected), ("v", grad_out), ("v", gain), *(("v", part) for part in all_stats)],
        [("v", (pixels, padded), BF16), ("v", (SUB, channels), F32)],
    )
    theirs = lax.ppermute(full, "slab", near)
    (own_product,) = call(product_kernel, [("v", full), ("v", depth)], [("v", (channels, channels), F32)])
    lines = -(-11 // pieces)
    batch = samples * copies
    if pieces == 4:
        share_outs = [("v", (share, channels), F32), ("v", (share, channels), BF16)]
    else:
        share_outs = [("v", (pieces // 2, share, channels), F32)]
    products = call(
        functools.partial(shares_kernel, pieces, share),
        [("s", where), ("v", theirs), ("v", other_depth), ("v", own_product)],
        share_outs,
        [pltpu.VMEM((channels, channels), F32)],
    )
    if pieces == 4:
        keep, leaving = products
    else:
        blocks = products[0]
        while blocks.shape[0] > 2:
            half = blocks.shape[0] // 2
            high = ((me // 2) & half) != 0
            mine = lax.dynamic_slice_in_dim(blocks, jnp.where(high, half, 0), half, 0)
            leaving = lax.dynamic_slice_in_dim(blocks, jnp.where(high, 0, half), half, 0).astype(BF16)
            came = lax.ppermute(leaving, "slab", [(i, i ^ (2 * half)) for i in range(pieces)])
            blocks = mine + came.astype(F32)
        bit = (me // 2) % 2
        keep = blocks[0] if pieces == 2 else lax.dynamic_index_in_dim(blocks, bit, 0, False)
        leaving = None if pieces == 2 else lax.dynamic_index_in_dim(blocks, 1 - bit, 0, False).astype(BF16)
    if pieces > 2:
        leaving, full = lax.optimization_barrier((leaving, full))
        came = lax.ppermute(leaving, "slab", across)
    else:
        came = jnp.zeros((share, channels), BF16)
    depth_grad, taps, edge_one, edge_two = call(
        functools.partial(backward_kernel, rows),
        [("s", where), ("v", full), ("o", point_weight), ("o", active)],
        [("a", lane3, F32), ("v", (2 * SUB, channels), F32), ("v", (cols, channels), BF16), ("v", (cols, channels), BF16)],
        [point_buf, buf3, buf3, DMA((3,))],
    )
    fold_outs = [("v", (lines, channels), F32)] * 2
    if pieces == 4:
        stay, leave = call(
            functools.partial(small_kernel, pieces),
            [("s", where), ("v", taps), ("v", lax.ppermute(taps, "slab", near)), ("v", norm)],
            fold_outs,
        )
        leave, norm = lax.optimization_barrier((leave, norm))
        leave = lax.ppermute(leave, "slab", across)
    else:
        all_taps = lax.all_gather(taps, "slab", axis=0, tiled=True)
        stay, leave = call(functools.partial(fold_kernel, pieces), [("s", where), ("v", all_taps), ("v", norm)], fold_outs)
    (block_out,) = call(
        functools.partial(block_kernel, rows),
        [("a", inputs), ("o", projected), ("v", norm), ("v", gain), ("v", shift)],
        [("v", (rows, flat), BF16)],
        [flat_buf, pltpu.VMEM((pixels, channels), F32), flat_f32, DMA((2,))],
    )
    stay, block_out = lax.optimization_barrier((stay, block_out))
    piece = -(-(share + 2 * lines) // copies)
    total = piece * copies
    (packed,) = call(
        pack_kernel,
        [("v", keep), ("v", came), ("v", stay), ("v", leave)],
        [("v", (copies, piece, channels), BF16)],
        [pltpu.VMEM((total, channels), F32)],
    )
    landed = lax.all_to_all(packed, "dp", 0, 0)
    (summed,) = call(total_kernel, [("v", landed)], [("v", packed.shape, BF16)])
    gathered = lax.all_to_all(summed, "dp", 0, 0)
    halo_one = lax.ppermute(edge_one, "slab", near)
    halo_two = lax.ppermute(edge_two, "slab", far)
    (grad_input,) = call(
        functools.partial(input_kernel, pieces, rows),
        [("s", where), ("a", class_weights), ("a", inputs), ("a", upstream), ("a", label_lines), ("a", depth_grad), ("v", halo_one), ("v", halo_two), ("a", depth_kernel)],
        [("v", (rows, flat), BF16)],
        [flat_buf, flat_buf, buf3, flat_f32, class_buf, label_buf, kernel_buf, weight_buf, DMA((6,))],
    )
    point_out, tap_out, gain_out, shift_out = call(
        functools.partial(unpack_kernel, pieces, batch),
        [("v", gathered)],
        [("v", (share, channels), F32), ("v", (9, share), F32), ("v", (share,), F32), ("v", (share,), F32)],
        [pltpu.VMEM((total, channels), F32)],
    )
    return (
        block_out.reshape(inputs.shape),
        grad_input.reshape(inputs.shape),
        point_out.T,
        tap_out,
        gain_out,
        shift_out,
    )


def solution(mesh):
    return jax.shard_map(
        local,
        mesh=mesh,
        in_specs=(
            P("dp", "slab", None),
            P("dp", "slab", None),
            P("dp", "slab", None),
            P(),
            P(),
            P(),
            P(),
            P(),
        ),
        out_specs=(
            P("dp", "slab", None),
            P("dp", "slab", None),
            P(None, "slab"),
            P(None, "slab"),
            P("slab"),
            P("slab"),
        ),
        check_vma=False,
    )
```
